32 devices in a mesh: wide: 8 (over z, y), narrow: 4 (over x, core).
Axes of the slice: x: 2, y: 2, z: 4, core: 2. Of those that a mesh axis runs over, the one named last changes fastest.
Arguments:
- loads: float32 [32, 8, 8, 512], P('wide', 'narrow'), may hold values from -6 to 6
- schur: float32 [32, 8, 512, 512], P('wide', 'narrow'), as said below
- local_inverse: float32 [32, 8, 512, 512], P('wide', 'narrow'), as said below
- coarse_basis: float32 [32, 8, 16, 512], P('wide', 'narrow'), may hold values from -0.6 to 0.6
- coarse_inverse: float32 [2176, 2176], P('wide', 'narrow'), may hold values from -0.125 to 0.125
- coarse_index: int32 [32, 8, 16], P('wide', 'narrow'), may hold values from 0 to 2175, as said below
Outputs:
- solution: float32 [32, 8, 8, 512], P('wide', 'narrow')
- residual: float32 [32, 8, 8, 512], P('wide', 'narrow')
The draws below stay inside these ranges and needn't reach their ends.
Inputs may be any that keep to these rules, and one draw needn't show every extreme that they name: `coarse_index`: the 4 coarse dofs of a face (local positions f * 4 to f * 4 + 3 for face f in the order west, east, south, north) carry one global number each; a face shared by two subdomains has the same numbers on both sides, and every number of 0 to 2175 belongs to exactly one face. `schur`: each subdomain's block is symmetric with a dominant positive diagonal. `local_inverse`: each subdomain's block is symmetric with a dominant positive diagonal.
All inputs are finite; a program needn't handle non-finite values.
Results may differ from the reference program's by a relative error of at most 0.0001.
Values sent between devices are 32-bit elements; how exact they have to be, the bound alone decides.
A program may use at most 128 MiB of HBM per device.

```python
import math
from functools import partial
import jax
import jax.numpy as jnp
from jax import lax

NI = 512
CF = 4
CD = 16
LOADS = 8
ITERS = 2
CIRC = 32
ACROSS = 8
COARSE = 2176


def dominant_block(sub_key, low, high, coupling, uniform_flag):
    first_key, second_key = jax.random.split(sub_key)
    diagonal = jnp.exp(jax.random.uniform(first_key, (NI,), jnp.float32, math.log(low), math.log(high)))
    if uniform_flag:
        random_part = jax.random.uniform(second_key, (NI, NI), jnp.float32, -1.7320508, 1.7320508)
    else:
        random_part = jax.random.normal(second_key, (NI, NI), jnp.float32)
    coupled = (random_part + random_part.T) * (coupling / math.sqrt(2.0 * NI))
    return coupled + jnp.diag(diagonal)


def draw_blocks(key, salt, low, high, coupling, uniform_flag):
    sub_keys = jax.random.split(jax.random.fold_in(key, salt), CIRC * ACROSS)
    maker = partial(dominant_block, low=low, high=high, coupling=coupling, uniform_flag=uniform_flag)
    stacked = lax.map(maker, sub_keys)
    return stacked.reshape(CIRC, ACROSS, NI, NI).astype(jnp.float32)


def draw_schur(key, part):
    return draw_blocks(key, 3, 1.0, 3.0, 0.3, False)


def draw_local_inverse(key, part):
    return draw_blocks(key, 5, 0.3, 1.0, 0.1, False)


def draw_coarse_index(key, part):
    face_order = jax.random.permutation(jax.random.fold_in(key, 7), CIRC * (2 * ACROSS + 1)).astype(jnp.int32)
    circ_pos = jnp.arange(CIRC, dtype=jnp.int32)[:, None]
    across_pos = jnp.arange(ACROSS, dtype=jnp.int32)[None, :]
    vertical_count = CIRC * ACROSS
    west_face = circ_pos * ACROSS + across_pos
    east_face = (circ_pos + 1) % CIRC * ACROSS + across_pos
    south_face = vertical_count + circ_pos * (ACROSS + 1) + across_pos
    north_face = south_face + 1
    faces = jnp.stack([west_face, east_face, south_face, north_face], axis=-1)
    numbers = face_order[faces][..., None] * CF + jnp.arange(CF, dtype=jnp.int32)
    return numbers.reshape(CIRC, ACROSS, CD).astype(jnp.int32)


def level_of(key, extent, cuts, least, high):
    def one(dim, parts):
        heights = jax.random.uniform(jax.random.fold_in(jax.random.fold_in(key, 6), dim), (parts,), jnp.float32, least / len(cuts), high / len(cuts))
        return jnp.repeat(jnp.exp(heights), extent[dim] // parts).reshape((-1,) + (1,) * (len(extent) - dim - 1))

    factor_of = one(*cuts[0])
    for cut in cuts[1:]:
        factor_of = factor_of * one(*cut)
    return factor_of


def normal_values(stream_key, shape, deviation, reach, pieces=(), held_as=jnp.bfloat16):
    entries = deviation * jax.random.normal(stream_key, shape, jnp.float32)
    if pieces:
        entries = entries * level_of(stream_key, shape, pieces, -0.22, 0.18)
    return jnp.clip(entries, -reach, reach).astype(held_as)


def setup_inputs(seed: int = 0) -> dict:
    key_of = jax.random.split(jax.random.key(seed), 7)
    return {
        "loads": normal_values(key_of[0], (CIRC, ACROSS, LOADS, NI), 1.0, 6.0, ((0, 8), (1, 4)), jnp.float32),
        "schur": draw_schur(jax.random.fold_in(key_of[6], 71), 0),
        "local_inverse": draw_local_inverse(jax.random.fold_in(key_of[6], 71), 0),
        "coarse_basis": normal_values(key_of[3], (CIRC, ACROSS, CD, NI), 0.1, 0.6, ((0, 8), (1, 4)), jnp.float32),
        "coarse_inverse": normal_values(key_of[4], (COARSE, COARSE), COARSE ** -0.5, 0.125, ((0, 8), (1, 4)), jnp.float32),
        "coarse_index": draw_coarse_index(jax.random.fold_in(key_of[6], 71), 0),
    }


def face_weights(position, total, face_width):
    south_weight = jnp.where(position == 0, 1.0, 0.5)
    north_weight = jnp.where(position == total - 1, 1.0, 0.5)
    halves = jnp.full((position.shape[0], face_width), 0.5, jnp.float32)
    ones_row = jnp.ones((position.shape[0], face_width), jnp.float32)
    return jnp.concatenate([halves, halves, south_weight[:, None] * ones_row, north_weight[:, None] * ones_row], axis=1)


def face_sum(field):
    face_width = field.shape[3] // 4
    west_part = field[..., 0:face_width]
    east_part = field[..., face_width:2 * face_width]
    south_part = field[..., 2 * face_width:3 * face_width]
    north_part = field[..., 3 * face_width:]
    new_west = west_part + jnp.roll(east_part, 1, axis=0)
    new_east = east_part + jnp.roll(west_part, -1, axis=0)
    zero_row = jnp.zeros_like(north_part[:, :1])
    new_south = south_part + jnp.concatenate([zero_row, north_part[:, :-1]], axis=1)
    new_north = north_part + jnp.concatenate([south_part[:, 1:], zero_row], axis=1)
    return jnp.concatenate([new_west, new_east, new_south, new_north], axis=3)


def apply_blocks(blocks, field):
    return jnp.einsum('abij,ablj->abli', blocks, field, precision=lax.Precision.HIGHEST)


def reference(loads, schur, local_inverse, coarse_basis, coarse_inverse, coarse_index):
    circ_count = loads.shape[0]
    across_count = loads.shape[1]
    load_count = loads.shape[2]
    face_width = loads.shape[3] // 4
    inv_mult = face_weights(jnp.arange(across_count, dtype=jnp.int32), across_count, face_width)[None, :, None, :]
    flat_index = coarse_index.reshape(-1).astype(jnp.int32)
    coarse_total = coarse_inverse.shape[0]
    solution = jnp.zeros_like(loads)
    for iteration in range(ITERS):
        current = face_sum(loads - apply_blocks(schur, solution))
        weighted = current * inv_mult
        restricted = jnp.einsum('abli,abki->labk', weighted, coarse_basis, precision=lax.Precision.HIGHEST)
        restricted = restricted.reshape(load_count, -1)
        coarse_rhs = jnp.zeros((load_count, coarse_total), jnp.float32).at[:, flat_index].add(restricted)
        coarse_sol = jnp.einsum('lc,rc->lr', coarse_rhs, coarse_inverse, precision=lax.Precision.HIGHEST)
        picked = coarse_sol[:, flat_index].reshape(load_count, circ_count, across_count, -1)
        correction = apply_blocks(local_inverse, weighted) + jnp.einsum('labk,abki->abli', picked, coarse_basis, precision=lax.Precision.HIGHEST)
        solution = solution + face_sum(correction) * inv_mult
    residual = face_sum(loads - apply_blocks(schur, solution))
    return solution, residual
```

```python
import functools

import jax
import jax.numpy as jnp
from jax import lax
from jax.experimental import pallas as pl
from jax.experimental.pallas import tpu as pltpu
from jax.sharding import PartitionSpec as P

ITERS = 2
MESH = pl.DeviceIdType.MESH
F32 = jnp.float32
BF16 = jnp.bfloat16
GROUP = 4
LANES = 128


def halves(value):
    high = value.astype(BF16).astype(F32)
    return high, value - high


def stacked(value):
    high, low = halves(value)
    return jnp.concatenate([high, low], axis=0).astype(BF16)


def dot(left, right):
    return jnp.dot(left, right, preferred_element_type=F32)


def dot_t(left, right):
    return lax.dot_general(left, right, (((1,), (1,)), ((), ())), preferred_element_type=F32)


def kernel(
    dims,
    loads_ref,
    schur_ref,
    local_ref,
    basis_ref,
    coarse_ref,
    index_ref,
    solution_ref,
    residual_ref,
    stage,
    local_parts,
    schur_parts,
    coarse_parts,
    picked_rows,
    select,
    basis_parts,
    field,
    weighted_parts,
    smoothed,
    low_faces,
    high_faces,
    south_faces,
    north_faces,
    numbers,
    gathered,
    partials,
    stage_sems,
    face_send,
    face_recv,
    all_send,
    all_recv,
):
    wide_count, narrow_count, sub_circ, sub_across, load_count, dofs, coarse_dofs, rows, columns = dims
    subs = sub_circ * sub_across
    devices = wide_count * narrow_count
    face = dofs // 4
    packed = subs * coarse_dofs
    row_pad = partials.shape[3]
    column_pad = coarse_parts.shape[1]
    wide = lax.axis_index("wide")
    narrow = lax.axis_index("narrow")
    me = wide * narrow_count + narrow
    west = lax.rem(wide + wide_count - 1, wide_count)
    east = lax.rem(wide + 1, wide_count)
    has_south = narrow > 0
    has_north = narrow < narrow_count - 1

    def stage_copy(source, s):
        return pltpu.make_async_copy(source.at[s], stage.at[s], stage_sems.at[s])

    for s in range(subs):
        stage_copy(local_ref, s).start()

    def place(flat):
        return (lax.div(flat, narrow_count), lax.rem(flat, narrow_count))

    barrier = pltpu.get_barrier_semaphore()

    def greet(step, carry):
        pl.semaphore_signal(
            barrier, inc=1, device_id=place(lax.rem(me + step, devices)), device_id_type=MESH
        )
        return carry

    south_faces[...] = jnp.zeros_like(south_faces)
    north_faces[...] = jnp.zeros_like(north_faces)
    numbers[pl.ds(me, 1)] = jnp.broadcast_to(index_ref[...], (1, 8, packed))
    lax.fori_loop(1, devices, greet, 0)

    coarse_parts[...] = jnp.zeros_like(coarse_parts)
    coarse_high, coarse_low = halves(coarse_ref[...])
    coarse_parts[0:rows, 0:columns] = coarse_high.astype(BF16)
    coarse_parts[rows : 2 * rows, 0:columns] = coarse_low.astype(BF16)
    basis_high, basis_low = halves(basis_ref[...])
    basis_parts[0] = basis_high.astype(BF16)
    basis_parts[1] = basis_low.astype(BF16)
    for iteration in range(ITERS):
        partials[iteration, pl.ds(me, 1)] = jnp.zeros((1, load_count, row_pad), F32)

    pl.semaphore_wait(barrier, devices - 1)

    def all_copy(buffer, turn, target):
        return pltpu.make_async_remote_copy(
            src_ref=buffer.at[me],
            dst_ref=buffer.at[me],
            send_sem=all_send.at[turn],
            recv_sem=all_recv.at[turn],
            device_id=target,
            device_id_type=MESH,
        )

    def send_all(buffer, turn):
        def body(step, carry):
            all_copy(buffer, turn, place(lax.rem(me + step, devices))).start()
            return carry

        lax.fori_loop(1, devices, body, 0)

    def others(buffer, turn):
        return pltpu.make_async_remote_copy(
            src_ref=buffer.at[pl.ds(0, devices - 1)],
            dst_ref=buffer.at[pl.ds(0, devices - 1)],
            send_sem=all_send.at[turn],
            recv_sem=all_recv.at[turn],
            device_id=place(lax.rem(me + 1, devices)),
            device_id_type=MESH,
        )

    def face_copies(source, turn):
        def copy(src, dst, send, recv, target):
            return pltpu.make_async_remote_copy(
                src_ref=src,
                dst_ref=dst.at[turn],
                send_sem=face_send.at[turn, send],
                recv_sem=face_recv.at[turn, recv],
                device_id=target,
                device_id_type=MESH,
            )

        to_west = copy(
            source.at[0, :, :, pl.ds(0, face)], high_faces, 0, 1, (west, narrow)
        )
        to_east = copy(
            source.at[sub_circ - 1, :, :, pl.ds(face, face)], low_faces, 1, 0, (east, narrow)
        )
        to_south = copy(
            source.at[:, 0, :, pl.ds(2 * face, face)],
            north_faces,
            2,
            3,
            (wide, jnp.maximum(narrow - 1, 0)),
        )
        to_north = copy(
            source.at[:, sub_across - 1, :, pl.ds(3 * face, face)],
            south_faces,
            3,
            2,
            (wide, jnp.minimum(narrow + 1, narrow_count - 1)),
        )
        return to_west, to_east, to_south, to_north

    def send_faces(source, turn):
        to_west, to_east, to_south, to_north = face_copies(source, turn)
        to_west.start()
        to_east.start()
        pl.when(has_south)(to_south.start)
        pl.when(has_north)(to_north.start)

    def wait_faces(source, turn):
        to_west, to_east, to_south, to_north = face_copies(source, turn)
        to_west.wait_recv()
        to_east.wait_recv()
        pl.when(has_north)(to_south.wait_recv)
        pl.when(has_south)(to_north.wait_recv)

    def drain_faces(source, turn):
        to_west, to_east, to_south, to_north = face_copies(source, turn)
        to_west.wait_send()
        to_east.wait_send()
        pl.when(has_south)(to_south.wait_send)
        pl.when(has_north)(to_north.wait_send)

    def summed(source, turn, a, b):
        own = source[a, b]
        low = source[a - 1, b, :, face : 2 * face] if a > 0 else low_faces[turn, b]
        high = source[a + 1, b, :, 0:face] if a < sub_circ - 1 else high_faces[turn, b]
        south = source[a, b - 1, :, 3 * face :] if b > 0 else south_faces[turn, a]
        north = (
            source[a, b + 1, :, 2 * face : 3 * face]
            if b < sub_across - 1
            else north_faces[turn, a]
        )
        return own + jnp.concatenate([low, high, south, north], axis=1)

    def inv_mult(b):
        south = jnp.where(has_south, 0.5, 1.0) if b == 0 else 0.5
        north = jnp.where(has_north, 0.5, 1.0) if b == sub_across - 1 else 0.5
        lane = lax.broadcasted_iota(jnp.int32, (1, dofs), 1)
        return jnp.where(lane >= 3 * face, north, jnp.where(lane >= 2 * face, south, 0.5))

    def split_stage(target):
        source = local_ref if target is local_parts else schur_ref

        def body(s, carry):
            stage_copy(source, s).wait()
            high, low = halves(stage[s])
            target[0, s] = high.astype(BF16)
            target[1, s] = low.astype(BF16)
            return carry

        lax.fori_loop(0, subs, body, 0)

    def apply_block(parts, s, vector):
        out = dot(vector, parts[0, s]) + dot(vector, parts[1, s])
        return out[0:load_count] + out[load_count:]

    send_faces(loads_ref, 0)
    send_all(numbers, 0)
    split_stage(local_parts)
    for s in range(subs):
        stage_copy(schur_ref, s).start()

    lane_sub = lax.broadcasted_iota(jnp.int32, (subs, load_count, packed), 2)
    own_sub = lax.broadcasted_iota(jnp.int32, (subs, load_count, packed), 0)
    mine = lax.div(lane_sub, coarse_dofs) == own_sub

    def make_operator():
        others(numbers, 0).wait_recv()
        row_ids = lax.broadcasted_iota(jnp.int32, (column_pad, GROUP * packed), 0)

        def body(group, carry):
            numbers_row = jnp.concatenate(
                [numbers[group * GROUP + p, 0:1] for p in range(GROUP)], axis=1
            )
            hot = (row_ids == numbers_row - narrow * columns).astype(F32).astype(BF16)
            picked_rows[group] = dot(coarse_parts[...], hot).astype(BF16)
            return carry

        lax.fori_loop(0, devices // GROUP, body, 0)
        block_ids = lax.broadcasted_iota(jnp.int32, (row_pad, packed), 0)

        def body_select(block, carry):
            local = index_ref[...] - block * rows
            select[block] = (
                ((block_ids == local) & (block_ids < rows)).astype(F32).astype(BF16)
            )
            return carry

        lax.fori_loop(0, wide_count, body_select, 0)

    def source_of(iteration):
        return loads_ref if iteration == 0 else field.at[2 * iteration - 1]

    for iteration in range(ITERS):
        turn = 2 * iteration
        source = source_of(iteration)
        wait_faces(source, turn)
        products = []
        for a in range(sub_circ):
            for b in range(sub_across):
                s = a * sub_across + b
                weighted = summed(source, turn, a, b) * inv_mult(b)
                parts = stacked(weighted)
                weighted_parts[s] = parts
                restricted = dot_t(parts, basis_parts[0]) + dot_t(parts, basis_parts[1])
                products.append(restricted[0:load_count] + restricted[load_count:])
        restricted = jnp.sum(jnp.where(mine, jnp.stack(products), 0.0), axis=0)
        gathered[iteration, pl.ds(me, 1)] = restricted[None]
        send_all(gathered.at[iteration], 1 + 2 * iteration)
        if iteration == 0:
            make_operator()
        for s in range(subs):
            smoothed[s] = apply_block(local_parts, s, weighted_parts[s])
        others(gathered.at[iteration], 1 + 2 * iteration).wait_recv()

        def add_group(group, total):
            vector = jnp.concatenate(
                [gathered[iteration, group * GROUP + p] for p in range(GROUP)], axis=1
            )
            return total + dot_t(stacked(vector), picked_rows[group])

        total = lax.fori_loop(
            0,
            devices // GROUP,
            add_group,
            jnp.zeros((2 * load_count, 2 * rows), F32),
        )
        total = total[0:load_count] + total[load_count:]
        total = total[:, 0:rows] + total[:, rows:]
        partials[iteration, pl.ds(me, 1), :, 0:rows] = total[None]
        send_all(partials.at[iteration], 2 + 2 * iteration)
        if iteration == 0:
            split_stage(schur_parts)
        others(partials.at[iteration], 2 + 2 * iteration).wait_recv()

        def add_block(block, total):
            coarse = partials[iteration, block * narrow_count]
            for n in range(1, narrow_count):
                coarse = coarse + partials[iteration, block * narrow_count + n]
            return total + dot(stacked(coarse), select[block])

        picked = lax.fori_loop(
            0, wide_count, add_block, jnp.zeros((2 * load_count, packed), F32)
        )
        picked = picked[0:load_count] + picked[load_count:]
        spread = jnp.where(mine, picked[None], 0.0).reshape(subs * load_count, packed)
        spread = stacked(spread)
        spread = dot(spread, basis_parts[0]) + dot(spread, basis_parts[1])
        spread = spread[0 : subs * load_count] + spread[subs * load_count :]
        for a in range(sub_circ):
            for b in range(sub_across):
                s = a * sub_across + b
                field[2 * iteration, a, b] = (
                    smoothed[s] + spread[s * load_count : (s + 1) * load_count]
                )
        correction = field.at[2 * iteration]
        send_faces(correction, turn + 1)
        wait_faces(correction, turn + 1)
        for a in range(sub_circ):
            for b in range(sub_across):
                s = a * sub_across + b
                update = summed(correction, turn + 1, a, b) * inv_mult(b)
                if iteration > 0:
                    update = update + solution_ref[a, b]
                solution_ref[a, b] = update
                field[2 * iteration + 1, a, b] = loads_ref[a, b] - apply_block(
                    schur_parts, s, stacked(update)
                )
        send_faces(field.at[2 * iteration + 1], turn + 2)

    last = source_of(ITERS)
    wait_faces(last, 2 * ITERS)
    for a in range(sub_circ):
        for b in range(sub_across):
            residual_ref[a, b] = summed(last, 2 * ITERS, a, b)

    others(numbers, 0).wait_send()
    for iteration in range(ITERS):
        others(gathered.at[iteration], 1 + 2 * iteration).wait_send()
        others(partials.at[iteration], 2 + 2 * iteration).wait_send()
    drain_faces(loads_ref, 0)
    for turn in range(2 * ITERS):
        drain_faces(field.at[turn], turn + 1)


def per_device(wide_count, narrow_count, loads, schur, local_inverse, coarse_basis, coarse_inverse, coarse_index):
    sub_circ, sub_across, load_count, dofs = loads.shape
    coarse_dofs = coarse_basis.shape[2]
    rows, columns = coarse_inverse.shape
    subs = sub_circ * sub_across
    packed = subs * coarse_dofs
    devices = wide_count * narrow_count
    face = dofs // 4
    row_pad = pl.cdiv(rows, LANES) * LANES
    column_pad = pl.cdiv(columns, LANES) * LANES
    turns = 2 * ITERS + 1
    dims = (wide_count, narrow_count, sub_circ, sub_across, load_count, dofs, coarse_dofs, rows, columns)
    vmem = pl.BlockSpec(memory_space=pltpu.VMEM)
    anywhere = pl.BlockSpec(memory_space=pl.ANY)
    shape = jax.ShapeDtypeStruct(loads.shape, F32)
    return tuple(
        pl.pallas_call(
            functools.partial(kernel, dims),
            out_shape=(shape, shape),
            in_specs=[vmem, anywhere, anywhere, vmem, vmem, vmem],
            out_specs=(vmem, vmem),
            scratch_shapes=[
                pltpu.VMEM((subs, dofs, dofs), F32),
                pltpu.VMEM((2, subs, dofs, dofs), BF16),
                pltpu.VMEM((2, subs, dofs, dofs), BF16),
                pltpu.VMEM((2 * rows, column_pad), BF16),
                pltpu.VMEM((devices // GROUP, 2 * rows, GROUP * packed), BF16),
                pltpu.VMEM((wide_count, row_pad, packed), BF16),
                pltpu.VMEM((2, packed, dofs), BF16),
                pltpu.VMEM((2 * ITERS, sub_circ, sub_across, load_count, dofs), F32),
                pltpu.VMEM((subs, 2 * load_count, dofs), BF16),
                pltpu.VMEM((subs, load_count, dofs), F32),
                pltpu.VMEM((turns, sub_across, load_count, face), F32),
                pltpu.VMEM((turns, sub_across, load_count, face), F32),
                pltpu.VMEM((turns, sub_circ, load_count, face), F32),
                pltpu.VMEM((turns, sub_circ, load_count, face), F32),
                pltpu.VMEM((devices, 8, packed), jnp.int32),
                pltpu.VMEM((ITERS, devices, load_count, packed), F32),
                pltpu.VMEM((ITERS, devices, load_count, row_pad), F32),
                pltpu.SemaphoreType.DMA((subs,)),
                pltpu.SemaphoreType.DMA((turns, 4)),
                pltpu.SemaphoreType.DMA((turns, 4)),
                pltpu.SemaphoreType.DMA((turns,)),
                pltpu.SemaphoreType.DMA((turns,)),
            ],
            compiler_params=pltpu.CompilerParams(
                collective_id=0, has_side_effects=True, vmem_limit_bytes=60 * 1024 * 1024
            ),
        )(
            loads,
            schur.reshape(subs, dofs, dofs),
            local_inverse.reshape(subs, dofs, dofs),
            coarse_basis.reshape(packed, dofs),
            coarse_inverse,
            coarse_index.reshape(1, packed),
        )
    )


def solution(mesh):
    return jax.shard_map(
        functools.partial(per_device, mesh.shape["wide"], mesh.shape["narrow"]),
        mesh=mesh,
        in_specs=(
            P("wide", "narrow", None, None),
            P("wide", "narrow", None, None),
            P("wide", "narrow", None, None),
            P("wide", "narrow", None, None),
            P("wide", "narrow"),
            P("wide", "narrow", None),
        ),
        out_specs=(P("wide", "narrow", None, None), P("wide", "narrow", None, None)),
        check_vma=False,
    )
```

```python
import functools

import jax
import jax.numpy as jnp
from jax import lax
from jax.experimental import pallas as pl
from jax.experimental.pallas import tpu as pltpu
from jax.sharding import PartitionSpec as P

ITERS = 2
MESH = pl.DeviceIdType.MESH
F32 = jnp.float32
BF16 = jnp.bfloat16
GROUP = 4
LANES = 128


def halves(value):
    high = value.astype(BF16).astype(F32)
    return high, value - high


def stacked(value):
    high, low = halves(value)
    return jnp.concatenate([high, low], axis=0).astype(BF16)


def dot(left, right):
    return jnp.dot(left, right, preferred_element_type=F32)


def dot_t(left, right):
    return lax.dot_general(left, right, (((1,), (1,)), ((), ())), preferred_element_type=F32)


def kernel(
    dims,
    loads_ref,
    schur_ref,
    local_ref,
    basis_ref,
    coarse_ref,
    index_ref,
    solution_ref,
    residual_ref,
    stage,
    local_parts,
    schur_parts,
    coarse_parts,
    picked_rows,
    select,
    basis_parts,
    halo_parts,
    halo_hoop,
    halo_across,
    field,
    correction,
    weighted_parts,
    smoothed,
    low_faces,
    high_faces,
    south_faces,
    north_faces,
    numbers,
    gathered,
    narrow_rows,
    wide_rows,
    stage_sems,
    face_send,
    face_recv,
    all_send,
    all_recv,
):
    wide_count, narrow_count, sub_circ, sub_across, load_count, dofs, coarse_dofs, rows, columns = dims
    subs = sub_circ * sub_across
    slots = stage.shape[0]
    devices = wide_count * narrow_count
    face = dofs // 4
    packed = subs * coarse_dofs
    row_pad = wide_rows.shape[3]
    column_pad = coarse_parts.shape[1]
    wide = lax.axis_index("wide")
    narrow = lax.axis_index("narrow")

    def wrapped(position, step, count):
        moved = position + step
        return jnp.where(moved >= count, moved - count, moved)

    west = wrapped(wide, wide_count - 1, wide_count)
    east = wrapped(wide, 1, wide_count)
    south = jnp.maximum(narrow - 1, 0)
    north = jnp.minimum(narrow + 1, narrow_count - 1)
    has_south = narrow > 0
    has_north = narrow < narrow_count - 1
    wide_peers = [(wrapped(wide, step, wide_count), narrow) for step in range(1, wide_count)]
    narrow_peers = [(wide, wrapped(narrow, step, narrow_count)) for step in range(1, narrow_count)]

    def stage_copy(source, s):
        q = s if source is local_ref else s + subs
        slot = lax.rem(q, slots)
        return pltpu.make_async_copy(source.at[s], stage.at[slot], stage_sems.at[slot])

    south_faces[...] = jnp.zeros_like(south_faces)
    north_faces[...] = jnp.zeros_like(north_faces)
    halo_hoop[...] = jnp.zeros_like(halo_hoop)
    halo_across[...] = jnp.zeros_like(halo_across)
    barrier = pltpu.get_barrier_semaphore()
    for peer in wide_peers + narrow_peers:
        pl.semaphore_signal(barrier, inc=1, device_id=peer, device_id_type=MESH)
    for s in range(slots):
        stage_copy(local_ref, s).start()

    index_row = jnp.concatenate(
        [index_ref[a, b : b + 1] for a in range(sub_circ) for b in range(sub_across)], axis=1
    )
    numbers[narrow, pl.ds(wide, 1)] = jnp.broadcast_to(index_row, (1, 8, packed))
    coarse_parts[...] = jnp.zeros_like(coarse_parts)
    coarse_high, coarse_low = halves(coarse_ref[...])
    coarse_parts[0:rows, 0:columns] = coarse_high.astype(BF16)
    coarse_parts[rows : 2 * rows, 0:columns] = coarse_low.astype(BF16)
    basis_high, basis_low = halves(basis_ref[...].reshape(packed, dofs))
    basis_parts[0] = basis_high.astype(BF16)
    basis_parts[1] = basis_low.astype(BF16)
    for iteration in range(ITERS):
        narrow_rows[iteration, pl.ds(narrow, 1)] = jnp.zeros((1, load_count, row_pad), F32)

    pl.semaphore_wait(barrier, len(wide_peers) + len(narrow_peers))

    def remote(src, dst, phase, peer):
        return pltpu.make_async_remote_copy(
            src_ref=src,
            dst_ref=dst,
            send_sem=all_send.at[phase],
            recv_sem=all_recv.at[phase],
            device_id=peer,
            device_id_type=MESH,
        )

    def send(block, phase, peers):
        for peer in peers:
            remote(block, block, phase, peer).start()

    def arrivals(slots, phase, peers):
        part = slots.at[pl.ds(0, len(peers))]
        return remote(part, part, phase, peers[0])

    def send_wide(buffer, phase):
        send(buffer.at[narrow, wide], phase, wide_peers)

    def send_narrow(buffer, phase):
        arrivals(buffer.at[narrow], phase, wide_peers).wait_recv()
        send(buffer.at[narrow], phase + 1, narrow_peers)

    def wait_narrow(buffer, phase):
        arrivals(buffer, phase + 1, narrow_peers).wait_recv()

    def face_copies(source, turn):
        def copy(src, dst, send, recv, target):
            return pltpu.make_async_remote_copy(
                src_ref=src,
                dst_ref=dst.at[turn],
                send_sem=face_send.at[turn, send],
                recv_sem=face_recv.at[turn, recv],
                device_id=target,
                device_id_type=MESH,
            )

        to_west = copy(
            source.at[0, :, :, pl.ds(0, face)], high_faces, 0, 1, (west, narrow)
        )
        to_east = copy(
            source.at[sub_circ - 1, :, :, pl.ds(face, face)], low_faces, 1, 0, (east, narrow)
        )
        to_south = copy(
            source.at[:, 0, :, pl.ds(2 * face, face)],
            north_faces,
            2,
            3,
            (wide, south),
        )
        to_north = copy(
            source.at[:, sub_across - 1, :, pl.ds(3 * face, face)],
            south_faces,
            3,
            2,
            (wide, north),
        )
        return to_west, to_east, to_south, to_north

    def halo_copies():
        turn = 2 * ITERS + 1

        def copy(src, dst, send, recv, target):
            return pltpu.make_async_remote_copy(
                src_ref=src,
                dst_ref=dst,
                send_sem=face_send.at[turn, send],
                recv_sem=face_recv.at[turn, recv],
                device_id=target,
                device_id_type=MESH,
            )

        first, last = 0, sub_across - 1
        return (
            copy(basis_ref.at[0, :, :, pl.ds(0, face)], halo_hoop.at[0], 0, 1, (west, narrow)),
            copy(
                basis_ref.at[sub_circ - 1, :, :, pl.ds(face, face)],
                halo_hoop.at[sub_circ - 1],
                1,
                0,
                (east, narrow),
            ),
            copy(
                basis_ref.at[:, first, :, pl.ds(2 * face, face)],
                halo_across.at[:, first],
                2,
                3,
                (wide, south),
            ),
            copy(
                basis_ref.at[:, last, :, pl.ds(3 * face, face)],
                halo_across.at[:, last],
                3,
                2,
                (wide, north),
            ),
        )

    def send_four(copies):
        to_west, to_east, to_south, to_north = copies
        to_west.start()
        to_east.start()
        pl.when(has_south)(to_south.start)
        pl.when(has_north)(to_north.start)

    def wait_four(copies):
        to_west, to_east, to_south, to_north = copies
        to_west.wait_recv()
        to_east.wait_recv()
        pl.when(has_north)(to_south.wait_recv)
        pl.when(has_south)(to_north.wait_recv)

    def drain_four(copies):
        to_west, to_east, to_south, to_north = copies
        to_west.wait_send()
        to_east.wait_send()
        pl.when(has_south)(to_south.wait_send)
        pl.when(has_north)(to_north.wait_send)

    def summed(source, turn, a, b, extra=None):
        def received(faces, which, i, x, y):
            if extra is None:
                return faces[turn, i]
            start = (x * sub_across + y) * load_count
            return faces[turn, i] + extra[which][start : start + load_count]

        own = source[a, b]
        low = (
            source[a - 1, b, :, face : 2 * face]
            if a > 0
            else received(low_faces, 0, b, sub_circ - 1, b)
        )
        high = (
            source[a + 1, b, :, 0:face]
            if a < sub_circ - 1
            else received(high_faces, 0, b, 0, b)
        )
        below = (
            source[a, b - 1, :, 3 * face :]
            if b > 0
            else received(south_faces, 1, a, a, sub_across - 1)
        )
        above = (
            source[a, b + 1, :, 2 * face : 3 * face]
            if b < sub_across - 1
            else received(north_faces, 1, a, a, 0)
        )
        return own + jnp.concatenate([low, high, below, above], axis=1)

    def inv_mult(b):
        below = jnp.where(has_south, 0.5, 1.0) if b == 0 else 0.5
        above = jnp.where(has_north, 0.5, 1.0) if b == sub_across - 1 else 0.5
        lane = lax.broadcasted_iota(jnp.int32, (1, dofs), 1)
        return jnp.where(lane >= 3 * face, above, jnp.where(lane >= 2 * face, below, 0.5))

    def split_stage(target):
        source = local_ref if target is local_parts else schur_ref

        def body(s, carry):
            stage_copy(source, s).wait()
            high, low = halves(stage[lax.rem(s if source is local_ref else s + subs, slots)])
            target[0, s] = high.astype(BF16)
            target[1, s] = low.astype(BF16)
            later = s + slots
            pl.when(later < subs)(lambda: stage_copy(source, later).start())
            if source is local_ref:
                pl.when(later >= subs)(lambda: stage_copy(schur_ref, later - subs).start())
            return carry

        lax.fori_loop(0, subs, body, 0)

    def apply_block(parts, s, vector):
        out = dot(vector, parts[0, s]) + dot(vector, parts[1, s])
        return out[0:load_count] + out[load_count:]

    send_four(face_copies(loads_ref, 0))
    send_wide(numbers, 0)
    send_four(halo_copies())
    split_stage(local_parts)
    send_narrow(numbers, 0)

    lane_sub = lax.broadcasted_iota(jnp.int32, (subs, load_count, packed), 2)
    own_sub = lax.broadcasted_iota(jnp.int32, (subs, load_count, packed), 0)
    mine = (lane_sub >= own_sub * coarse_dofs) & (lane_sub < (own_sub + 1) * coarse_dofs)
    groups = devices // GROUP
    per_row = wide_count // GROUP

    def make_operator():
        wait_narrow(numbers, 0)
        row_ids = lax.broadcasted_iota(jnp.int32, (column_pad, GROUP * packed), 0)

        def body(group, carry):
            n = lax.div(group, per_row)
            w = lax.rem(group, per_row) * GROUP
            numbers_row = jnp.concatenate([numbers[n, w + p, 0:1] for p in range(GROUP)], axis=1)
            hot = (row_ids == numbers_row - narrow * columns).astype(F32).astype(BF16)
            picked_rows[group] = dot(coarse_parts[...], hot).astype(BF16)
            return carry

        lax.fori_loop(0, groups, body, 0)
        block_ids = lax.broadcasted_iota(jnp.int32, (row_pad, 3 * packed), 0)
        lane = lax.broadcasted_iota(jnp.int32, (1, packed), 1)
        hoop = jnp.where(
            lane < sub_across * coarse_dofs, numbers[narrow, east, 0:1], numbers[narrow, west, 0:1]
        )
        lane_across = lax.rem(lane, sub_across * coarse_dofs)
        across = jnp.where(
            lane_across < coarse_dofs, numbers[north, wide, 0:1], numbers[south, wide, 0:1]
        )
        wanted = jnp.concatenate([numbers[narrow, wide, 0:1], hoop, across], axis=1)

        def body_select(block, carry):
            hot = (block_ids == wanted - block * rows) & (block_ids < rows)
            select[block] = hot.astype(F32).astype(BF16)
            return carry

        lax.fori_loop(0, wide_count, body_select, 0)
        wait_four(halo_copies())
        for source, target in ((halo_hoop, 0), (halo_across, 1)):
            high, low = halves(source[...].reshape(packed, face))
            halo_parts[target, 0] = high.astype(BF16)
            halo_parts[target, 1] = low.astype(BF16)

    def spread(values, parts):
        rows_of = stacked(jnp.where(mine, values[None], 0.0).reshape(subs * load_count, packed))
        out = dot(rows_of, parts[0]) + dot(rows_of, parts[1])
        return out[0 : subs * load_count] + out[subs * load_count :]

    def smooth(first, last):
        for s in range(first, last):
            smoothed[iteration, s // sub_across, s % sub_across] = apply_block(
                local_parts, s, weighted_parts[s]
            )

    def unroll_of(count):
        return min(count, 8)

    for iteration in range(ITERS):
        turn = 2 * iteration
        phase = 2 + 4 * iteration
        source = loads_ref if iteration == 0 else field.at[iteration - 1]
        coarse_in = gathered.at[iteration]
        wait_four(face_copies(source, turn))
        for a in range(sub_circ):
            for b in range(sub_across):
                weighted = summed(source, turn, a, b) * inv_mult(b)
                weighted_parts[a * sub_across + b] = stacked(weighted)
        flat = weighted_parts[...].reshape(subs * 2 * load_count, dofs)
        products = dot_t(flat, basis_parts[0]) + dot_t(flat, basis_parts[1])
        products = products.reshape(subs, 2, load_count, packed)
        products = products[:, 0] + products[:, 1]
        restricted = jnp.sum(jnp.where(mine, products, 0.0), axis=0)
        coarse_in[narrow, pl.ds(wide, 1)] = restricted[None]
        send_wide(coarse_in, phase)
        smooth(0, subs // 2)
        send_narrow(coarse_in, phase)
        smooth(subs // 2, subs)
        send_four(face_copies(smoothed.at[iteration], turn + 1))
        if iteration == 0:
            make_operator()
        wait_narrow(coarse_in, phase)

        def add_group(group, total):
            n = lax.div(group, per_row)
            w = lax.rem(group, per_row) * GROUP
            vector = jnp.concatenate([coarse_in[n, w + p] for p in range(GROUP)], axis=1)
            return total + dot_t(stacked(vector), picked_rows[group])

        total = lax.fori_loop(
            0,
            groups,
            add_group,
            jnp.zeros((2 * load_count, 2 * rows), F32),
            unroll=unroll_of(groups),
        )
        total = total[0:load_count] + total[load_count:]
        total = total[:, 0:rows] + total[:, rows:]
        narrow_rows[iteration, pl.ds(narrow, 1), :, 0:rows] = total[None]
        send(narrow_rows.at[iteration, narrow], phase + 2, narrow_peers)
        if iteration == 0:
            split_stage(schur_parts)
        arrivals(narrow_rows.at[iteration], phase + 2, narrow_peers).wait_recv()
        wide_rows[iteration, pl.ds(wide, 1)] = jnp.sum(
            narrow_rows[iteration], axis=0, keepdims=True
        )
        send(wide_rows.at[iteration, wide], phase + 3, wide_peers)
        wait_four(face_copies(smoothed.at[iteration], turn + 1))
        arrivals(wide_rows.at[iteration], phase + 3, wide_peers).wait_recv()

        def add_block(block, total):
            return total + dot(stacked(wide_rows[iteration, block]), select[block])

        picked = lax.fori_loop(
            0,
            wide_count,
            add_block,
            jnp.zeros((2 * load_count, 3 * packed), F32),
            unroll=unroll_of(wide_count),
        )
        picked = picked[0:load_count] + picked[load_count:]
        inner = spread(picked[:, 0:packed], basis_parts)
        extra = (
            spread(picked[:, packed : 2 * packed], halo_parts[0]),
            spread(picked[:, 2 * packed :], halo_parts[1]),
        )
        for a in range(sub_circ):
            for b in range(sub_across):
                start = (a * sub_across + b) * load_count
                correction[a, b] = smoothed[iteration, a, b] + inner[start : start + load_count]
        for a in range(sub_circ):
            for b in range(sub_across):
                update = summed(correction, turn + 1, a, b, extra) * inv_mult(b)
                if iteration > 0:
                    update = update + solution_ref[a, b]
                solution_ref[a, b] = update
                field[iteration, a, b] = loads_ref[a, b] - apply_block(
                    schur_parts, a * sub_across + b, stacked(update)
                )
        send_four(face_copies(field.at[iteration], turn + 2))

    last = field.at[ITERS - 1]
    wait_four(face_copies(last, 2 * ITERS))
    for a in range(sub_circ):
        for b in range(sub_across):
            residual_ref[a, b] = summed(last, 2 * ITERS, a, b)

    arrivals(numbers.at[narrow], 0, wide_peers).wait_send()
    arrivals(numbers, 1, narrow_peers).wait_send()
    for iteration in range(ITERS):
        phase = 2 + 4 * iteration
        arrivals(gathered.at[iteration, narrow], phase, wide_peers).wait_send()
        arrivals(gathered.at[iteration], phase + 1, narrow_peers).wait_send()
        arrivals(narrow_rows.at[iteration], phase + 2, narrow_peers).wait_send()
        arrivals(wide_rows.at[iteration], phase + 3, wide_peers).wait_send()
        drain_four(face_copies(smoothed.at[iteration], 2 * iteration + 1))
        drain_four(face_copies(field.at[iteration], 2 * iteration + 2))
    drain_four(face_copies(loads_ref, 0))
    drain_four(halo_copies())


def per_device(wide_count, narrow_count, loads, schur, local_inverse, coarse_basis, coarse_inverse, coarse_index):
    sub_circ, sub_across, load_count, dofs = loads.shape
    coarse_dofs = coarse_basis.shape[2]
    rows, columns = coarse_inverse.shape
    subs = sub_circ * sub_across
    packed = subs * coarse_dofs
    devices = wide_count * narrow_count
    face = dofs // 4
    row_pad = pl.cdiv(rows, LANES) * LANES
    column_pad = pl.cdiv(columns, LANES) * LANES
    turns = 2 * ITERS + 1
    slots = max(1, subs - 3)
    dims = (wide_count, narrow_count, sub_circ, sub_across, load_count, dofs, coarse_dofs, rows, columns)
    vmem = pl.BlockSpec(memory_space=pltpu.VMEM)
    anywhere = pl.BlockSpec(memory_space=pl.ANY)
    shape = jax.ShapeDtypeStruct(loads.shape, F32)
    return tuple(
        pl.pallas_call(
            functools.partial(kernel, dims),
            out_shape=(shape, shape),
            in_specs=[vmem, anywhere, anywhere, vmem, vmem, vmem],
            out_specs=(vmem, vmem),
            scratch_shapes=[
                pltpu.VMEM((slots, dofs, dofs), F32),
                pltpu.VMEM((2, subs, dofs, dofs), BF16),
                pltpu.VMEM((2, subs, dofs, dofs), BF16),
                pltpu.VMEM((2 * rows, column_pad), BF16),
                pltpu.VMEM((devices // GROUP, 2 * rows, GROUP * packed), BF16),
                pltpu.VMEM((wide_count, row_pad, 3 * packed), BF16),
                pltpu.VMEM((2, packed, dofs), BF16),
                pltpu.VMEM((2, 2, packed, face), BF16),
                pltpu.VMEM((sub_circ, sub_across, coarse_dofs, face), F32),
                pltpu.VMEM((sub_circ, sub_across, coarse_dofs, face), F32),
                pltpu.VMEM((ITERS, *loads.shape), F32),
                pltpu.VMEM(loads.shape, F32),
                pltpu.VMEM((subs, 2 * load_count, dofs), BF16),
                pltpu.VMEM((ITERS, *loads.shape), F32),
                pltpu.VMEM((turns, sub_across, load_count, face), F32),
                pltpu.VMEM((turns, sub_across, load_count, face), F32),
                pltpu.VMEM((turns, sub_circ, load_count, face), F32),
                pltpu.VMEM((turns, sub_circ, load_count, face), F32),
                pltpu.VMEM((narrow_count, wide_count, 8, packed), jnp.int32),
                pltpu.VMEM((ITERS, narrow_count, wide_count, load_count, packed), F32),
                pltpu.VMEM((ITERS, narrow_count, load_count, row_pad), F32),
                pltpu.VMEM((ITERS, wide_count, load_count, row_pad), F32),
                pltpu.SemaphoreType.DMA((slots,)),
                pltpu.SemaphoreType.DMA((turns + 1, 4)),
                pltpu.SemaphoreType.DMA((turns + 1, 4)),
                pltpu.SemaphoreType.DMA((4 * ITERS + 2,)),
                pltpu.SemaphoreType.DMA((4 * ITERS + 2,)),
            ],
            compiler_params=pltpu.CompilerParams(
                collective_id=0, has_side_effects=True, vmem_limit_bytes=60 * 1024 * 1024
            ),
        )(
            loads,
            schur.reshape(subs, dofs, dofs),
            local_inverse.reshape(subs, dofs, dofs),
            coarse_basis,
            coarse_inverse,
            coarse_index,
        )
    )


def solution(mesh):
    return jax.shard_map(
        functools.partial(per_device, mesh.shape["wide"], mesh.shape["narrow"]),
        mesh=mesh,
        in_specs=(
            P("wide", "narrow", None, None),
            P("wide", "narrow", None, None),
            P("wide", "narrow", None, None),
            P("wide", "narrow", None, None),
            P("wide", "narrow"),
            P("wide", "narrow", None),
        ),
        out_specs=(P("wide", "narrow", None, None), P("wide", "narrow", None, None)),
        check_vma=False,
    )
```

```python
import functools

import jax
import jax.numpy as jnp
from jax import lax
from jax.experimental import pallas as pl
from jax.experimental.pallas import tpu as pltpu
from jax.sharding import PartitionSpec as P

ITERS = 2
MESH = pl.DeviceIdType.MESH
F32 = jnp.float32
BF16 = jnp.bfloat16
GROUP = 4
HOT_BYTES = 8 * 1024 * 1024
LANES = 128


def halves(value):
    high = value.astype(BF16).astype(F32)
    return high, value - high


def stacked(value):
    high, low = halves(value)
    return jnp.concatenate([high, low], axis=0).astype(BF16)


def dot(left, right):
    return jnp.dot(left, right, preferred_element_type=F32)


def dot_t(left, right):
    return lax.dot_general(left, right, (((1,), (1,)), ((), ())), preferred_element_type=F32)


def kernel(
    dims,
    loads_ref,
    schur_ref,
    local_ref,
    basis_ref,
    coarse_ref,
    index_ref,
    solution_ref,
    residual_ref,
    stage,
    local_parts,
    schur_parts,
    coarse_parts,
    hot,
    select,
    basis_parts,
    halo_parts,
    halo_hoop,
    halo_across,
    field,
    correction,
    weighted_parts,
    smoothed,
    low_faces,
    high_faces,
    south_faces,
    north_faces,
    numbers,
    numbers_across,
    gathered,
    pieces_out,
    pieces_in,
    narrow_rows,
    wide_rows,
    stage_sems,
    face_send,
    face_recv,
    all_send,
    all_recv,
):
    wide_count, narrow_count, sub_circ, sub_across, load_count, dofs, coarse_dofs, rows, columns = dims
    subs = sub_circ * sub_across
    slots = stage.shape[0]
    devices = wide_count * narrow_count
    face = dofs // 4
    packed = subs * coarse_dofs
    row_pad = wide_rows.shape[3]
    column_pad = coarse_parts.shape[1]
    wide = lax.axis_index("wide")
    narrow = lax.axis_index("narrow")

    def wrapped(position, step, count):
        moved = position + step
        return jnp.where(moved >= count, moved - count, moved)

    west = wrapped(wide, wide_count - 1, wide_count)
    east = wrapped(wide, 1, wide_count)
    south = jnp.maximum(narrow - 1, 0)
    north = jnp.minimum(narrow + 1, narrow_count - 1)
    has_south = narrow > 0
    has_north = narrow < narrow_count - 1
    wide_peers = [(wrapped(wide, step, wide_count), narrow) for step in range(1, wide_count)]
    narrow_peers = [(wide, wrapped(narrow, step, narrow_count)) for step in range(1, narrow_count)]

    def stage_copy(source, s):
        q = s if source is local_ref else s + subs
        slot = lax.rem(q, slots)
        return pltpu.make_async_copy(source.at[s], stage.at[slot], stage_sems.at[slot])

    south_faces[...] = jnp.zeros_like(south_faces)
    north_faces[...] = jnp.zeros_like(north_faces)
    halo_hoop[...] = jnp.zeros_like(halo_hoop)
    halo_across[...] = jnp.zeros_like(halo_across)
    barrier = pltpu.get_barrier_semaphore()
    for peer in wide_peers + narrow_peers:
        pl.semaphore_signal(barrier, inc=1, device_id=peer, device_id_type=MESH)
    for s in range(slots):
        stage_copy(local_ref, s).start()

    index_row = jnp.concatenate(
        [index_ref[a, b : b + 1] for a in range(sub_circ) for b in range(sub_across)], axis=1
    )
    numbers[pl.ds(wide, 1)] = jnp.broadcast_to(index_row, (1, 8, packed))
    numbers_across[pl.ds(narrow, 1)] = jnp.broadcast_to(index_row, (1, 8, packed))
    coarse_parts[...] = jnp.zeros_like(coarse_parts)
    coarse_high, coarse_low = halves(coarse_ref[...])
    coarse_parts[0:rows, 0:columns] = coarse_high.astype(BF16)
    coarse_parts[rows : 2 * rows, 0:columns] = coarse_low.astype(BF16)
    basis_high, basis_low = halves(basis_ref[...].reshape(packed, dofs))
    basis_parts[0] = basis_high.astype(BF16)
    basis_parts[1] = basis_low.astype(BF16)
    for iteration in range(ITERS):
        narrow_rows[iteration, pl.ds(narrow, 1)] = jnp.zeros((1, load_count, row_pad), F32)

    pl.semaphore_wait(barrier, len(wide_peers) + len(narrow_peers))

    def remote(src, dst, phase, peer):
        return pltpu.make_async_remote_copy(
            src_ref=src,
            dst_ref=dst,
            send_sem=all_send.at[phase],
            recv_sem=all_recv.at[phase],
            device_id=peer,
            device_id_type=MESH,
        )

    def send(block, phase, peers):
        for peer in peers:
            remote(block, block, phase, peer).start()

    def arrivals(slots, phase, peers):
        part = slots.at[pl.ds(0, len(peers))]
        return remote(part, part, phase, peers[0])

    def face_copies(source, turn):
        def copy(src, dst, send, recv, target):
            return pltpu.make_async_remote_copy(
                src_ref=src,
                dst_ref=dst.at[turn],
                send_sem=face_send.at[turn, send],
                recv_sem=face_recv.at[turn, recv],
                device_id=target,
                device_id_type=MESH,
            )

        to_west = copy(
            source.at[0, :, :, pl.ds(0, face)], high_faces, 0, 1, (west, narrow)
        )
        to_east = copy(
            source.at[sub_circ - 1, :, :, pl.ds(face, face)], low_faces, 1, 0, (east, narrow)
        )
        to_south = copy(
            source.at[:, 0, :, pl.ds(2 * face, face)],
            north_faces,
            2,
            3,
            (wide, south),
        )
        to_north = copy(
            source.at[:, sub_across - 1, :, pl.ds(3 * face, face)],
            south_faces,
            3,
            2,
            (wide, north),
        )
        return to_west, to_east, to_south, to_north

    def halo_copies():
        turn = 2 * ITERS + 1

        def copy(src, dst, send, recv, target):
            return pltpu.make_async_remote_copy(
                src_ref=src,
                dst_ref=dst,
                send_sem=face_send.at[turn, send],
                recv_sem=face_recv.at[turn, recv],
                device_id=target,
                device_id_type=MESH,
            )

        first, last = 0, sub_across - 1
        return (
            copy(basis_ref.at[0, :, :, pl.ds(0, face)], halo_hoop.at[0], 0, 1, (west, narrow)),
            copy(
                basis_ref.at[sub_circ - 1, :, :, pl.ds(face, face)],
                halo_hoop.at[sub_circ - 1],
                1,
                0,
                (east, narrow),
            ),
            copy(
                basis_ref.at[:, first, :, pl.ds(2 * face, face)],
                halo_across.at[:, first],
                2,
                3,
                (wide, south),
            ),
            copy(
                basis_ref.at[:, last, :, pl.ds(3 * face, face)],
                halo_across.at[:, last],
                3,
                2,
                (wide, north),
            ),
        )

    def send_four(copies):
        to_west, to_east, to_south, to_north = copies
        to_west.start()
        to_east.start()
        pl.when(has_south)(to_south.start)
        pl.when(has_north)(to_north.start)

    def wait_four(copies):
        to_west, to_east, to_south, to_north = copies
        to_west.wait_recv()
        to_east.wait_recv()
        pl.when(has_north)(to_south.wait_recv)
        pl.when(has_south)(to_north.wait_recv)

    def drain_four(copies):
        to_west, to_east, to_south, to_north = copies
        to_west.wait_send()
        to_east.wait_send()
        pl.when(has_south)(to_south.wait_send)
        pl.when(has_north)(to_north.wait_send)

    def summed(source, turn, a, b, extra=None):
        def received(faces, which, i, x, y):
            if extra is None:
                return faces[turn, i]
            start = (x * sub_across + y) * load_count
            return faces[turn, i] + extra[which][start : start + load_count]

        own = source[a, b]
        low = (
            source[a - 1, b, :, face : 2 * face]
            if a > 0
            else received(low_faces, 0, b, sub_circ - 1, b)
        )
        high = (
            source[a + 1, b, :, 0:face]
            if a < sub_circ - 1
            else received(high_faces, 0, b, 0, b)
        )
        below = (
            source[a, b - 1, :, 3 * face :]
            if b > 0
            else received(south_faces, 1, a, a, sub_across - 1)
        )
        above = (
            source[a, b + 1, :, 2 * face : 3 * face]
            if b < sub_across - 1
            else received(north_faces, 1, a, a, 0)
        )
        return own + jnp.concatenate([low, high, below, above], axis=1)

    def inv_mult(b):
        below = jnp.where(has_south, 0.5, 1.0) if b == 0 else 0.5
        above = jnp.where(has_north, 0.5, 1.0) if b == sub_across - 1 else 0.5
        lane = lax.broadcasted_iota(jnp.int32, (1, dofs), 1)
        return jnp.where(lane >= 3 * face, above, jnp.where(lane >= 2 * face, below, 0.5))

    def split_stage(target):
        source = local_ref if target is local_parts else schur_ref

        def body(s, carry):
            stage_copy(source, s).wait()
            high, low = halves(stage[lax.rem(s if source is local_ref else s + subs, slots)])
            target[0, s] = high.astype(BF16)
            target[1, s] = low.astype(BF16)
            later = s + slots
            pl.when(later < subs)(lambda: stage_copy(source, later).start())
            if source is local_ref:
                pl.when(later >= subs)(lambda: stage_copy(schur_ref, later - subs).start())
            return carry

        lax.fori_loop(0, subs, body, 0)

    def apply_block(parts, s, vector):
        out = dot(vector, parts[0, s]) + dot(vector, parts[1, s])
        return out[0:load_count] + out[load_count:]

    send_four(face_copies(loads_ref, 0))
    send(numbers.at[wide], 0, wide_peers)
    send(numbers_across.at[narrow], 1, narrow_peers)
    send_four(halo_copies())
    split_stage(local_parts)

    lane_sub = lax.broadcasted_iota(jnp.int32, (subs, load_count, packed), 2)
    own_sub = lax.broadcasted_iota(jnp.int32, (subs, load_count, packed), 0)
    mine = (lane_sub >= own_sub * coarse_dofs) & (lane_sub < (own_sub + 1) * coarse_dofs)
    groups = wide_count // GROUP
    stored = hot.shape[0] == groups
    hot_ids = lax.broadcasted_iota(jnp.int32, (column_pad, GROUP * packed), 0)

    def fill(group, slot, n):
        row = jnp.concatenate([numbers[group * GROUP + p, 0:1] for p in range(GROUP)], axis=1)
        hot[slot, n] = (hot_ids == row - n * columns).astype(F32).astype(BF16)

    def make_hot():
        arrivals(numbers, 0, wide_peers).wait_recv()
        if stored:
            for group in range(groups):
                for n in range(narrow_count):
                    fill(group, group, n)

    def make_select():
        arrivals(numbers_across, 1, narrow_peers).wait_recv()
        block_ids = lax.broadcasted_iota(jnp.int32, (row_pad, 3 * packed), 0)
        lane = lax.broadcasted_iota(jnp.int32, (1, packed), 1)
        hoop = jnp.where(
            lane < sub_across * coarse_dofs, numbers[east, 0:1], numbers[west, 0:1]
        )
        lane_across = lax.rem(lane, sub_across * coarse_dofs)
        across = jnp.where(
            lane_across < coarse_dofs, numbers_across[north, 0:1], numbers_across[south, 0:1]
        )
        wanted = jnp.concatenate([numbers[wide, 0:1], hoop, across], axis=1)

        def body_select(block, carry):
            hot = (block_ids == wanted - block * rows) & (block_ids < rows)
            select[block] = hot.astype(F32).astype(BF16)
            return carry

        lax.fori_loop(0, wide_count, body_select, 0)
        wait_four(halo_copies())
        for source, target in ((halo_hoop, 0), (halo_across, 1)):
            high, low = halves(source[...].reshape(packed, face))
            halo_parts[target, 0] = high.astype(BF16)
            halo_parts[target, 1] = low.astype(BF16)

    def spread(values, parts):
        rows_of = stacked(jnp.where(mine, values[None], 0.0).reshape(subs * load_count, packed))
        out = dot(rows_of, parts[0]) + dot(rows_of, parts[1])
        return out[0 : subs * load_count] + out[subs * load_count :]

    def smooth(first, last):
        for s in range(first, last):
            smoothed[iteration, s // sub_across, s % sub_across] = apply_block(
                local_parts, s, weighted_parts[s]
            )

    def unroll_of(count):
        return min(count, 8)

    for iteration in range(ITERS):
        turn = 2 * iteration
        phase = 2 + 4 * iteration
        source = loads_ref if iteration == 0 else field.at[iteration - 1]
        coarse_in = gathered.at[iteration]
        wait_four(face_copies(source, turn))
        for a in range(sub_circ):
            for b in range(sub_across):
                weighted = summed(source, turn, a, b) * inv_mult(b)
                weighted_parts[a * sub_across + b] = stacked(weighted)
        flat = weighted_parts[...].reshape(subs * 2 * load_count, dofs)
        products = dot_t(flat, basis_parts[0]) + dot_t(flat, basis_parts[1])
        products = products.reshape(subs, 2, load_count, packed)
        products = products[:, 0] + products[:, 1]
        restricted = jnp.sum(jnp.where(mine, products, 0.0), axis=0)
        coarse_in[pl.ds(wide, 1)] = restricted[None]
        send(coarse_in.at[wide], phase, wide_peers)
        if iteration == 0:
            make_hot()
            smooth(0, subs)
        else:
            smooth(0, subs // 2)
        arrivals(coarse_in, phase, wide_peers).wait_recv()

        def add_group(group, totals):
            vector = jnp.concatenate([coarse_in[group * GROUP + p] for p in range(GROUP)], axis=1)
            vector = stacked(vector)
            sums = []
            for n in range(narrow_count):
                if not stored:
                    fill(group, 0, n)
                sums.append(totals[n] + dot_t(vector, hot[group if stored else 0, n]))
            return tuple(sums)

        totals = lax.fori_loop(
            0,
            groups,
            add_group,
            tuple(jnp.zeros((2 * load_count, column_pad), F32) for _ in range(narrow_count)),
            unroll=groups if stored else 1,
        )
        for n in range(narrow_count):
            pieces_out[iteration, n] = totals[n][0:load_count] + totals[n][load_count:]
        for peer in narrow_peers:
            remote(
                pieces_out.at[iteration, peer[1]], pieces_in.at[iteration, narrow], phase + 1, peer
            ).start()
        pieces_in[iteration, pl.ds(narrow, 1)] = pieces_out[iteration, pl.ds(narrow, 1)]
        if iteration == 0:
            make_select()
        else:
            smooth(subs // 2, subs)
        send_four(face_copies(smoothed.at[iteration], turn + 1))
        arrivals(pieces_in.at[iteration], phase + 1, narrow_peers).wait_recv()
        total = dot_t(stacked(jnp.sum(pieces_in[iteration], axis=0)), coarse_parts[...])
        total = total[0:load_count] + total[load_count:]
        total = total[:, 0:rows] + total[:, rows:]
        narrow_rows[iteration, pl.ds(narrow, 1), :, 0:rows] = total[None]
        send(narrow_rows.at[iteration, narrow], phase + 2, narrow_peers)
        if iteration == 0:
            split_stage(schur_parts)
        arrivals(narrow_rows.at[iteration], phase + 2, narrow_peers).wait_recv()
        wide_rows[iteration, pl.ds(wide, 1)] = jnp.sum(
            narrow_rows[iteration], axis=0, keepdims=True
        )
        send(wide_rows.at[iteration, wide], phase + 3, wide_peers)
        wait_four(face_copies(smoothed.at[iteration], turn + 1))
        arrivals(wide_rows.at[iteration], phase + 3, wide_peers).wait_recv()

        def add_block(block, total):
            return total + dot(stacked(wide_rows[iteration, block]), select[block])

        picked = lax.fori_loop(
            0,
            wide_count,
            add_block,
            jnp.zeros((2 * load_count, 3 * packed), F32),
            unroll=unroll_of(wide_count),
        )
        picked = picked[0:load_count] + picked[load_count:]
        inner = spread(picked[:, 0:packed], basis_parts)
        extra = (
            spread(picked[:, packed : 2 * packed], halo_parts[0]),
            spread(picked[:, 2 * packed :], halo_parts[1]),
        )
        for a in range(sub_circ):
            for b in range(sub_across):
                start = (a * sub_across + b) * load_count
                correction[a, b] = smoothed[iteration, a, b] + inner[start : start + load_count]
        for a in range(sub_circ):
            for b in range(sub_across):
                update = summed(correction, turn + 1, a, b, extra) * inv_mult(b)
                if iteration > 0:
                    update = update + solution_ref[a, b]
                solution_ref[a, b] = update
                field[iteration, a, b] = loads_ref[a, b] - apply_block(
                    schur_parts, a * sub_across + b, stacked(update)
                )
        send_four(face_copies(field.at[iteration], turn + 2))

    last = field.at[ITERS - 1]
    wait_four(face_copies(last, 2 * ITERS))
    for a in range(sub_circ):
        for b in range(sub_across):
            residual_ref[a, b] = summed(last, 2 * ITERS, a, b)

    arrivals(numbers, 0, wide_peers).wait_send()
    arrivals(numbers_across, 1, narrow_peers).wait_send()
    for iteration in range(ITERS):
        phase = 2 + 4 * iteration
        arrivals(gathered.at[iteration], phase, wide_peers).wait_send()
        arrivals(pieces_in.at[iteration], phase + 1, narrow_peers).wait_send()
        arrivals(narrow_rows.at[iteration], phase + 2, narrow_peers).wait_send()
        arrivals(wide_rows.at[iteration], phase + 3, wide_peers).wait_send()
        drain_four(face_copies(smoothed.at[iteration], 2 * iteration + 1))
        drain_four(face_copies(field.at[iteration], 2 * iteration + 2))
    drain_four(face_copies(loads_ref, 0))
    drain_four(halo_copies())


def hand_on(solution_in, residual_in, solution_out, residual_out, sems):
    copies = [
        pltpu.make_async_copy(solution_in, solution_out, sems.at[0]),
        pltpu.make_async_copy(residual_in, residual_out, sems.at[1]),
    ]
    for copy in copies:
        copy.start()
    for copy in copies:
        copy.wait()


def per_device(wide_count, narrow_count, loads, schur, local_inverse, coarse_basis, coarse_inverse, coarse_index):
    sub_circ, sub_across, load_count, dofs = loads.shape
    coarse_dofs = coarse_basis.shape[2]
    rows, columns = coarse_inverse.shape
    subs = sub_circ * sub_across
    packed = subs * coarse_dofs
    devices = wide_count * narrow_count
    face = dofs // 4
    row_pad = pl.cdiv(rows, LANES) * LANES
    column_pad = pl.cdiv(columns, LANES) * LANES
    turns = 2 * ITERS + 1
    slots = subs
    hot_bytes = wide_count * packed * narrow_count * column_pad * 2
    hot_slots = wide_count // GROUP if hot_bytes <= HOT_BYTES else 1
    dims = (wide_count, narrow_count, sub_circ, sub_across, load_count, dofs, coarse_dofs, rows, columns)
    vmem = pl.BlockSpec(memory_space=pltpu.VMEM)
    anywhere = pl.BlockSpec(memory_space=pl.ANY)
    shape = jax.ShapeDtypeStruct(loads.shape, F32)
    results = (
        pl.pallas_call(
            functools.partial(kernel, dims),
            out_shape=(shape, shape),
            in_specs=[vmem, anywhere, anywhere, vmem, vmem, vmem],
            out_specs=(vmem, vmem),
            scratch_shapes=[
                pltpu.VMEM((slots, dofs, dofs), F32),
                pltpu.VMEM((2, subs, dofs, dofs), BF16),
                pltpu.VMEM((2, subs, dofs, dofs), BF16),
                pltpu.VMEM((2 * rows, column_pad), BF16),
                pltpu.VMEM((hot_slots, narrow_count, column_pad, GROUP * packed), BF16),
                pltpu.VMEM((wide_count, row_pad, 3 * packed), BF16),
                pltpu.VMEM((2, packed, dofs), BF16),
                pltpu.VMEM((2, 2, packed, face), BF16),
                pltpu.VMEM((sub_circ, sub_across, coarse_dofs, face), F32),
                pltpu.VMEM((sub_circ, sub_across, coarse_dofs, face), F32),
                pltpu.VMEM((ITERS, *loads.shape), F32),
                pltpu.VMEM(loads.shape, F32),
                pltpu.VMEM((subs, 2 * load_count, dofs), BF16),
                pltpu.VMEM((ITERS, *loads.shape), F32),
                pltpu.VMEM((turns, sub_across, load_count, face), F32),
                pltpu.VMEM((turns, sub_across, load_count, face), F32),
                pltpu.VMEM((turns, sub_circ, load_count, face), F32),
                pltpu.VMEM((turns, sub_circ, load_count, face), F32),
                pltpu.VMEM((wide_count, 8, packed), jnp.int32),
                pltpu.VMEM((narrow_count, 8, packed), jnp.int32),
                pltpu.VMEM((ITERS, wide_count, load_count, packed), F32),
                pltpu.VMEM((ITERS, narrow_count, load_count, column_pad), F32),
                pltpu.VMEM((ITERS, narrow_count, load_count, column_pad), F32),
                pltpu.VMEM((ITERS, narrow_count, load_count, row_pad), F32),
                pltpu.VMEM((ITERS, wide_count, load_count, row_pad), F32),
                pltpu.SemaphoreType.DMA((slots,)),
                pltpu.SemaphoreType.DMA((turns + 1, 4)),
                pltpu.SemaphoreType.DMA((turns + 1, 4)),
                pltpu.SemaphoreType.DMA((4 * ITERS + 2,)),
                pltpu.SemaphoreType.DMA((4 * ITERS + 2,)),
            ],
            compiler_params=pltpu.CompilerParams(
                collective_id=0, has_side_effects=True, vmem_limit_bytes=60 * 1024 * 1024
            ),
        )(
            loads,
            schur.reshape(subs, dofs, dofs),
            local_inverse.reshape(subs, dofs, dofs),
            coarse_basis,
            coarse_inverse,
            coarse_index,
        )
    )
    return tuple(
        pl.pallas_call(
            hand_on,
            out_shape=(shape, shape),
            in_specs=[anywhere, anywhere],
            out_specs=(anywhere, anywhere),
            scratch_shapes=[pltpu.SemaphoreType.DMA((2,))],
            compiler_params=pltpu.CompilerParams(vmem_limit_bytes=60 * 1024 * 1024),
        )(*results)
    )


def solution(mesh):
    return jax.shard_map(
        functools.partial(per_device, mesh.shape["wide"], mesh.shape["narrow"]),
        mesh=mesh,
        in_specs=(
            P("wide", "narrow", None, None),
            P("wide", "narrow", None, None),
            P("wide", "narrow", None, None),
            P("wide", "narrow", None, None),
            P("wide", "narrow"),
            P("wide", "narrow", None),
        ),
        out_specs=(P("wide", "narrow", None, None), P("wide", "narrow", None, None)),
        check_vma=False,
    )
```

```python
import functools

import jax
import jax.numpy as jnp
from jax import lax
from jax.experimental import pallas as pl
from jax.experimental.pallas import tpu as pltpu
from jax.sharding import PartitionSpec as P

ITERS = 2
MESH = pl.DeviceIdType.MESH
F32 = jnp.float32
BF16 = jnp.bfloat16
GROUP = 4
HOT_BYTES = 8 * 1024 * 1024
LANES = 128


def halves(value):
    high = value.astype(BF16).astype(F32)
    return high, value - high


def stacked(value):
    high, low = halves(value)
    return jnp.concatenate([high, low], axis=0).astype(BF16)


def dot(left, right):
    return jnp.dot(left, right, preferred_element_type=F32)


def dot_t(left, right):
    return lax.dot_general(left, right, (((1,), (1,)), ((), ())), preferred_element_type=F32)


def kernel(
    dims,
    loads_ref,
    schur_ref,
    local_ref,
    basis_ref,
    coarse_ref,
    index_ref,
    solution_ref,
    residual_ref,
    stage,
    local_parts,
    schur_parts,
    coarse_parts,
    hot,
    select,
    basis_parts,
    halo_parts,
    halo_hoop,
    halo_across,
    field,
    correction,
    weighted_parts,
    smoothed,
    low_faces,
    high_faces,
    south_faces,
    north_faces,
    numbers,
    numbers_across,
    gathered,
    pieces_out,
    pieces_in,
    narrow_rows,
    wide_rows,
    stage_sems,
    face_send,
    face_recv,
    all_send,
    all_recv,
):
    wide_count, narrow_count, sub_circ, sub_across, load_count, dofs, coarse_dofs, rows, columns = dims
    subs = sub_circ * sub_across
    slots = stage.shape[0]
    devices = wide_count * narrow_count
    face = dofs // 4
    packed = subs * coarse_dofs
    row_pad = wide_rows.shape[3]
    column_pad = coarse_parts.shape[1]
    wide = lax.axis_index("wide")
    narrow = lax.axis_index("narrow")

    def wrapped(position, step, count):
        moved = position + step
        return jnp.where(moved >= count, moved - count, moved)

    west = wrapped(wide, wide_count - 1, wide_count)
    east = wrapped(wide, 1, wide_count)
    south = jnp.maximum(narrow - 1, 0)
    north = jnp.minimum(narrow + 1, narrow_count - 1)
    has_south = narrow > 0
    has_north = narrow < narrow_count - 1
    wide_peers = [(wrapped(wide, step, wide_count), narrow) for step in range(1, wide_count)]
    narrow_peers = [(wide, wrapped(narrow, step, narrow_count)) for step in range(1, narrow_count)]

    def stage_copy(source, s):
        q = s if source is local_ref else s + subs
        slot = lax.rem(q, slots)
        return pltpu.make_async_copy(source.at[s], stage.at[slot], stage_sems.at[slot])

    south_faces[...] = jnp.zeros_like(south_faces)
    north_faces[...] = jnp.zeros_like(north_faces)
    halo_hoop[...] = jnp.zeros_like(halo_hoop)
    halo_across[...] = jnp.zeros_like(halo_across)
    barrier = pltpu.get_barrier_semaphore()
    for peer in wide_peers + narrow_peers:
        pl.semaphore_signal(barrier, inc=1, device_id=peer, device_id_type=MESH)
    for s in range(slots):
        stage_copy(local_ref, s).start()

    index_row = jnp.concatenate(
        [index_ref[a, b : b + 1] for a in range(sub_circ) for b in range(sub_across)], axis=1
    )
    numbers[pl.ds(wide, 1)] = jnp.broadcast_to(index_row, (1, 8, packed))
    numbers_across[pl.ds(narrow, 1)] = jnp.broadcast_to(index_row, (1, 8, packed))
    coarse_parts[...] = jnp.zeros_like(coarse_parts)
    coarse_high, coarse_low = halves(coarse_ref[...])
    coarse_parts[0:rows, 0:columns] = coarse_high.astype(BF16)
    coarse_parts[rows : 2 * rows, 0:columns] = coarse_low.astype(BF16)
    basis_high, basis_low = halves(basis_ref[...].reshape(packed, dofs))
    basis_parts[0] = basis_high.astype(BF16)
    basis_parts[1] = basis_low.astype(BF16)
    pieces_out[...] = jnp.zeros_like(pieces_out)
    for iteration in range(ITERS):
        narrow_rows[iteration, pl.ds(narrow, 1)] = jnp.zeros((1, load_count, row_pad), F32)

    pl.semaphore_wait(barrier, len(wide_peers) + len(narrow_peers))

    def remote(src, dst, phase, peer):
        return pltpu.make_async_remote_copy(
            src_ref=src,
            dst_ref=dst,
            send_sem=all_send.at[phase],
            recv_sem=all_recv.at[phase],
            device_id=peer,
            device_id_type=MESH,
        )

    def send(block, phase, peers):
        for peer in peers:
            remote(block, block, phase, peer).start()

    def arrivals(slots, phase, peers):
        part = slots.at[pl.ds(0, len(peers))]
        return remote(part, part, phase, peers[0])

    def face_copies(source, turn):
        def copy(src, dst, send, recv, target):
            return pltpu.make_async_remote_copy(
                src_ref=src,
                dst_ref=dst.at[turn],
                send_sem=face_send.at[turn, send],
                recv_sem=face_recv.at[turn, recv],
                device_id=target,
                device_id_type=MESH,
            )

        to_west = copy(
            source.at[0, :, :, pl.ds(0, face)], high_faces, 0, 1, (west, narrow)
        )
        to_east = copy(
            source.at[sub_circ - 1, :, :, pl.ds(face, face)], low_faces, 1, 0, (east, narrow)
        )
        to_south = copy(
            source.at[:, 0, :, pl.ds(2 * face, face)],
            north_faces,
            2,
            3,
            (wide, south),
        )
        to_north = copy(
            source.at[:, sub_across - 1, :, pl.ds(3 * face, face)],
            south_faces,
            3,
            2,
            (wide, north),
        )
        return to_west, to_east, to_south, to_north

    def halo_copies():
        turn = 2 * ITERS + 1

        def copy(src, dst, send, recv, target):
            return pltpu.make_async_remote_copy(
                src_ref=src,
                dst_ref=dst,
                send_sem=face_send.at[turn, send],
                recv_sem=face_recv.at[turn, recv],
                device_id=target,
                device_id_type=MESH,
            )

        first, last = 0, sub_across - 1
        return (
            copy(basis_ref.at[0, :, :, pl.ds(0, face)], halo_hoop.at[0], 0, 1, (west, narrow)),
            copy(
                basis_ref.at[sub_circ - 1, :, :, pl.ds(face, face)],
                halo_hoop.at[sub_circ - 1],
                1,
                0,
                (east, narrow),
            ),
            copy(
                basis_ref.at[:, first, :, pl.ds(2 * face, face)],
                halo_across.at[:, first],
                2,
                3,
                (wide, south),
            ),
            copy(
                basis_ref.at[:, last, :, pl.ds(3 * face, face)],
                halo_across.at[:, last],
                3,
                2,
                (wide, north),
            ),
        )

    def send_four(copies):
        to_west, to_east, to_south, to_north = copies
        to_west.start()
        to_east.start()
        pl.when(has_south)(to_south.start)
        pl.when(has_north)(to_north.start)

    def wait_four(copies):
        to_west, to_east, to_south, to_north = copies
        to_west.wait_recv()
        to_east.wait_recv()
        pl.when(has_north)(to_south.wait_recv)
        pl.when(has_south)(to_north.wait_recv)

    def drain_four(copies):
        to_west, to_east, to_south, to_north = copies
        to_west.wait_send()
        to_east.wait_send()
        pl.when(has_south)(to_south.wait_send)
        pl.when(has_north)(to_north.wait_send)

    def summed(source, turn, a, b, extra=None):
        def received(faces, which, i, x, y):
            if extra is None:
                return faces[turn, i]
            start = (x * sub_across + y) * load_count
            return faces[turn, i] + extra[which][start : start + load_count]

        own = source[a, b]
        low = (
            source[a - 1, b, :, face : 2 * face]
            if a > 0
            else received(low_faces, 0, b, sub_circ - 1, b)
        )
        high = (
            source[a + 1, b, :, 0:face]
            if a < sub_circ - 1
            else received(high_faces, 0, b, 0, b)
        )
        below = (
            source[a, b - 1, :, 3 * face :]
            if b > 0
            else received(south_faces, 1, a, a, sub_across - 1)
        )
        above = (
            source[a, b + 1, :, 2 * face : 3 * face]
            if b < sub_across - 1
            else received(north_faces, 1, a, a, 0)
        )
        return own + jnp.concatenate([low, high, below, above], axis=1)

    def inv_mult(b):
        below = jnp.where(has_south, 0.5, 1.0) if b == 0 else 0.5
        above = jnp.where(has_north, 0.5, 1.0) if b == sub_across - 1 else 0.5
        lane = lax.broadcasted_iota(jnp.int32, (1, dofs), 1)
        return jnp.where(lane >= 3 * face, above, jnp.where(lane >= 2 * face, below, 0.5))

    def split_stage(target):
        source = local_ref if target is local_parts else schur_ref

        def body(s, carry):
            stage_copy(source, s).wait()
            high, low = halves(stage[lax.rem(s if source is local_ref else s + subs, slots)])
            target[0, s] = high.astype(BF16)
            target[1, s] = low.astype(BF16)
            later = s + slots
            pl.when(later < subs)(lambda: stage_copy(source, later).start())
            if source is local_ref:
                pl.when(later >= subs)(lambda: stage_copy(schur_ref, later - subs).start())
            return carry

        lax.fori_loop(0, subs, body, 0)

    def apply_block(parts, s, vector):
        out = dot(vector, parts[0, s]) + dot(vector, parts[1, s])
        return out[0:load_count] + out[load_count:]

    send_four(face_copies(loads_ref, 0))
    send(numbers.at[wide], 0, wide_peers)
    send(numbers_across.at[narrow], 1, narrow_peers)
    send_four(halo_copies())
    split_stage(local_parts)

    lane_sub = lax.broadcasted_iota(jnp.int32, (subs, load_count, packed), 2)
    own_sub = lax.broadcasted_iota(jnp.int32, (subs, load_count, packed), 0)
    mine = (lane_sub >= own_sub * coarse_dofs) & (lane_sub < (own_sub + 1) * coarse_dofs)
    groups = wide_count // GROUP
    stored = hot.shape[0] == groups
    hot_ids = lax.broadcasted_iota(jnp.int32, (columns, GROUP * packed), 0)

    def fill(group, slot):
        row = jnp.concatenate([numbers[group * GROUP + p, 0:1] for p in range(GROUP)], axis=1)
        for n in range(narrow_count):
            block = (hot_ids == row - n * columns).astype(F32).astype(BF16)
            hot[slot, n * columns : (n + 1) * columns] = block

    def make_hot():
        arrivals(numbers, 0, wide_peers).wait_recv()
        if stored:
            for group in range(groups):
                fill(group, group)

    def make_select():
        arrivals(numbers_across, 1, narrow_peers).wait_recv()
        block_ids = lax.broadcasted_iota(jnp.int32, (rows, 3 * packed), 0)
        lane = lax.broadcasted_iota(jnp.int32, (1, packed), 1)
        hoop = jnp.where(
            lane < sub_across * coarse_dofs, numbers[east, 0:1], numbers[west, 0:1]
        )
        lane_across = lax.rem(lane, sub_across * coarse_dofs)
        across = jnp.where(
            lane_across < coarse_dofs, numbers_across[north, 0:1], numbers_across[south, 0:1]
        )
        wanted = jnp.concatenate([numbers[wide, 0:1], hoop, across], axis=1)

        for block in range(wide_count):
            chosen = (block_ids == wanted - block * rows).astype(F32).astype(BF16)
            select[block * rows : (block + 1) * rows] = chosen
        wait_four(halo_copies())
        for source, target in ((halo_hoop, 0), (halo_across, 1)):
            high, low = halves(source[...].reshape(packed, face))
            halo_parts[target, 0] = high.astype(BF16)
            halo_parts[target, 1] = low.astype(BF16)

    def spread(values, parts):
        rows_of = stacked(jnp.where(mine, values[None], 0.0).reshape(subs * load_count, packed))
        out = dot(rows_of, parts[0]) + dot(rows_of, parts[1])
        return out[0 : subs * load_count] + out[subs * load_count :]

    cut = subs // 3

    def smooth(first, last):
        for s in range(first, last):
            smoothed[iteration, s // sub_across, s % sub_across] = apply_block(
                local_parts, s, weighted_parts[s]
            )

    for iteration in range(ITERS):
        turn = 2 * iteration
        phase = 2 + 4 * iteration
        source = loads_ref if iteration == 0 else field.at[iteration - 1]
        coarse_in = gathered.at[iteration]
        wait_four(face_copies(source, turn))
        for a in range(sub_circ):
            for b in range(sub_across):
                weighted = summed(source, turn, a, b) * inv_mult(b)
                weighted_parts[a * sub_across + b] = stacked(weighted)
        flat = weighted_parts[...].reshape(subs * 2 * load_count, dofs)
        products = dot_t(flat, basis_parts[0]) + dot_t(flat, basis_parts[1])
        products = products.reshape(subs, 2, load_count, packed)
        products = products[:, 0] + products[:, 1]
        restricted = jnp.sum(jnp.where(mine, products, 0.0), axis=0)
        coarse_in[pl.ds(wide, 1)] = restricted[None]
        send(coarse_in.at[wide], phase, wide_peers)
        if iteration == 0:
            make_hot()
        smooth(0, cut)
        arrivals(coarse_in, phase, wide_peers).wait_recv()

        def add_group(group, total):
            vector = jnp.concatenate([coarse_in[group * GROUP + p] for p in range(GROUP)], axis=1)
            if not stored:
                fill(group, 0)
            return total + dot_t(stacked(vector), hot[group if stored else 0])

        total = lax.fori_loop(
            0,
            groups,
            add_group,
            jnp.zeros((2 * load_count, narrow_count * columns), F32),
            unroll=groups if stored else 1,
        )
        total = total[0:load_count] + total[load_count:]
        for n in range(narrow_count):
            pieces_out[iteration, n, :, 0:columns] = total[:, n * columns : (n + 1) * columns]
        for peer in narrow_peers:
            remote(
                pieces_out.at[iteration, peer[1]], pieces_in.at[iteration, narrow], phase + 1, peer
            ).start()
        pieces_in[iteration, pl.ds(narrow, 1)] = pieces_out[iteration, pl.ds(narrow, 1)]
        smooth(cut, 2 * cut)
        if iteration == 0:
            make_select()
        arrivals(pieces_in.at[iteration], phase + 1, narrow_peers).wait_recv()
        total = dot_t(stacked(jnp.sum(pieces_in[iteration], axis=0)), coarse_parts[...])
        total = total[0:load_count] + total[load_count:]
        total = total[:, 0:rows] + total[:, rows:]
        narrow_rows[iteration, pl.ds(narrow, 1), :, 0:rows] = total[None]
        send(narrow_rows.at[iteration, narrow], phase + 2, narrow_peers)
        smooth(2 * cut, subs)
        send_four(face_copies(smoothed.at[iteration], turn + 1))
        arrivals(narrow_rows.at[iteration], phase + 2, narrow_peers).wait_recv()
        wide_rows[iteration, pl.ds(wide, 1)] = jnp.sum(
            narrow_rows[iteration], axis=0, keepdims=True
        )
        send(wide_rows.at[iteration, wide], phase + 3, wide_peers)
        if iteration == 0:
            split_stage(schur_parts)
        wait_four(face_copies(smoothed.at[iteration], turn + 1))
        arrivals(wide_rows.at[iteration], phase + 3, wide_peers).wait_recv()

        coarse = jnp.concatenate(
            [wide_rows[iteration, block, :, 0:rows] for block in range(wide_count)], axis=1
        )
        picked = dot(stacked(coarse), select[...])
        picked = picked[0:load_count] + picked[load_count:]
        inner = spread(picked[:, 0:packed], basis_parts)
        extra = (
            spread(picked[:, packed : 2 * packed], halo_parts[0]),
            spread(picked[:, 2 * packed :], halo_parts[1]),
        )
        for a in range(sub_circ):
            for b in range(sub_across):
                start = (a * sub_across + b) * load_count
                correction[a, b] = smoothed[iteration, a, b] + inner[start : start + load_count]
        to_west, to_east, to_south, to_north = face_copies(field.at[iteration], turn + 2)
        for a in [0, sub_circ - 1, *range(1, sub_circ - 1)]:
            for b in range(sub_across):
                update = summed(correction, turn + 1, a, b, extra) * inv_mult(b)
                if iteration > 0:
                    update = update + solution_ref[a, b]
                solution_ref[a, b] = update
                field[iteration, a, b] = loads_ref[a, b] - apply_block(
                    schur_parts, a * sub_across + b, stacked(update)
                )
            if a == 0:
                to_west.start()
            if a == sub_circ - 1:
                to_east.start()
        pl.when(has_south)(to_south.start)
        pl.when(has_north)(to_north.start)

    last = field.at[ITERS - 1]
    wait_four(face_copies(last, 2 * ITERS))
    for a in range(sub_circ):
        for b in range(sub_across):
            residual_ref[a, b] = summed(last, 2 * ITERS, a, b)

    arrivals(numbers, 0, wide_peers).wait_send()
    arrivals(numbers_across, 1, narrow_peers).wait_send()
    for iteration in range(ITERS):
        phase = 2 + 4 * iteration
        arrivals(gathered.at[iteration], phase, wide_peers).wait_send()
        arrivals(pieces_in.at[iteration], phase + 1, narrow_peers).wait_send()
        arrivals(narrow_rows.at[iteration], phase + 2, narrow_peers).wait_send()
        arrivals(wide_rows.at[iteration], phase + 3, wide_peers).wait_send()
        drain_four(face_copies(smoothed.at[iteration], 2 * iteration + 1))
        drain_four(face_copies(field.at[iteration], 2 * iteration + 2))
    drain_four(face_copies(loads_ref, 0))
    drain_four(halo_copies())


def hand_on(solution_in, residual_in, solution_out, residual_out):
    solution_out[...] = solution_in[...]
    residual_out[...] = residual_in[...]


def per_device(wide_count, narrow_count, loads, schur, local_inverse, coarse_basis, coarse_inverse, coarse_index):
    sub_circ, sub_across, load_count, dofs = loads.shape
    coarse_dofs = coarse_basis.shape[2]
    rows, columns = coarse_inverse.shape
    subs = sub_circ * sub_across
    packed = subs * coarse_dofs
    devices = wide_count * narrow_count
    face = dofs // 4
    row_pad = pl.cdiv(rows, LANES) * LANES
    column_pad = pl.cdiv(columns, LANES) * LANES
    turns = 2 * ITERS + 1
    slots = subs
    hot_bytes = wide_count * packed * narrow_count * columns * 2
    hot_slots = wide_count // GROUP if hot_bytes <= HOT_BYTES else 1
    dims = (wide_count, narrow_count, sub_circ, sub_across, load_count, dofs, coarse_dofs, rows, columns)
    vmem = pl.BlockSpec(memory_space=pltpu.VMEM)
    anywhere = pl.BlockSpec(memory_space=pl.ANY)
    shape = jax.ShapeDtypeStruct(loads.shape, F32)
    results = (
        pl.pallas_call(
            functools.partial(kernel, dims),
            out_shape=(shape, shape),
            in_specs=[vmem, anywhere, anywhere, vmem, vmem, vmem],
            out_specs=(vmem, vmem),
            scratch_shapes=[
                pltpu.VMEM((slots, dofs, dofs), F32),
                pltpu.VMEM((2, subs, dofs, dofs), BF16),
                pltpu.VMEM((2, subs, dofs, dofs), BF16),
                pltpu.VMEM((2 * rows, column_pad), BF16),
                pltpu.VMEM((hot_slots, narrow_count * columns, GROUP * packed), BF16),
                pltpu.VMEM((wide_count * rows, 3 * packed), BF16),
                pltpu.VMEM((2, packed, dofs), BF16),
                pltpu.VMEM((2, 2, packed, face), BF16),
                pltpu.VMEM((sub_circ, sub_across, coarse_dofs, face), F32),
                pltpu.VMEM((sub_circ, sub_across, coarse_dofs, face), F32),
                pltpu.VMEM((ITERS, *loads.shape), F32),
                pltpu.VMEM(loads.shape, F32),
                pltpu.VMEM((subs, 2 * load_count, dofs), BF16),
                pltpu.VMEM((ITERS, *loads.shape), F32),
                pltpu.VMEM((turns, sub_across, load_count, face), F32),
                pltpu.VMEM((turns, sub_across, load_count, face), F32),
                pltpu.VMEM((turns, sub_circ, load_count, face), F32),
                pltpu.VMEM((turns, sub_circ, load_count, face), F32),
                pltpu.VMEM((wide_count, 8, packed), jnp.int32),
                pltpu.VMEM((narrow_count, 8, packed), jnp.int32),
                pltpu.VMEM((ITERS, wide_count, load_count, packed), F32),
                pltpu.VMEM((ITERS, narrow_count, load_count, column_pad), F32),
                pltpu.VMEM((ITERS, narrow_count, load_count, column_pad), F32),
                pltpu.VMEM((ITERS, narrow_count, load_count, row_pad), F32),
                pltpu.VMEM((ITERS, wide_count, load_count, row_pad), F32),
                pltpu.SemaphoreType.DMA((slots,)),
                pltpu.SemaphoreType.DMA((turns + 1, 4)),
                pltpu.SemaphoreType.DMA((turns + 1, 4)),
                pltpu.SemaphoreType.DMA((4 * ITERS + 2,)),
                pltpu.SemaphoreType.DMA((4 * ITERS + 2,)),
            ],
            compiler_params=pltpu.CompilerParams(
                collective_id=0, has_side_effects=True, vmem_limit_bytes=60 * 1024 * 1024
            ),
        )(
            loads,
            schur.reshape(subs, dofs, dofs),
            local_inverse.reshape(subs, dofs, dofs),
            coarse_basis,
            coarse_inverse,
            coarse_index,
        )
    )
    return tuple(
        pl.pallas_call(
            hand_on,
            out_shape=(shape, shape),
            in_specs=[vmem, vmem],
            out_specs=(vmem, vmem),
            compiler_params=pltpu.CompilerParams(vmem_limit_bytes=60 * 1024 * 1024),
        )(*results)
    )


def solution(mesh):
    return jax.shard_map(
        functools.partial(per_device, mesh.shape["wide"], mesh.shape["narrow"]),
        mesh=mesh,
        in_specs=(
            P("wide", "narrow", None, None),
            P("wide", "narrow", None, None),
            P("wide", "narrow", None, None),
            P("wide", "narrow", None, None),
            P("wide", "narrow"),
            P("wide", "narrow", None),
        ),
        out_specs=(P("wide", "narrow", None, None), P("wide", "narrow", None, None)),
        check_vma=False,
    )
```

```python
import functools

import jax
import jax.numpy as jnp
from jax import lax
from jax.experimental import pallas as pl
from jax.experimental.pallas import tpu as pltpu
from jax.sharding import PartitionSpec as P

ITERS = 2
MESH = pl.DeviceIdType.MESH
F32 = jnp.float32
BF16 = jnp.bfloat16
GROUP = 4
HOT_BYTES = 8 * 1024 * 1024
LANES = 128


def halves(value):
    high = value.astype(BF16).astype(F32)
    return high, value - high


def stacked(value):
    high, low = halves(value)
    return jnp.concatenate([high, low], axis=0).astype(BF16)


def dot(left, right):
    return jnp.dot(left, right, preferred_element_type=F32)


def kernel(
    dims,
    loads_hbm,
    schur_ref,
    local_ref,
    basis_hbm,
    coarse_hbm,
    index_ref,
    solution_ref,
    residual_ref,
    loads_ref,
    basis_ref,
    coarse_ref,
    coarse_padded,
    stage,
    local_parts,
    schur_parts,
    coarse_parts,
    hot,
    select,
    basis_parts,
    basis_turned,
    halo_parts,
    halo_hoop,
    halo_across,
    field,
    correction,
    weighted_parts,
    smoothed,
    low_faces,
    high_faces,
    south_faces,
    north_faces,
    numbers,
    numbers_across,
    gathered,
    pieces_out,
    pieces_in,
    narrow_rows,
    wide_rows,
    stage_sems,
    input_sems,
    face_send,
    face_recv,
    all_send,
    all_recv,
):
    wide_count, narrow_count, sub_circ, sub_across, load_count, dofs, coarse_dofs, rows, columns = dims
    subs = sub_circ * sub_across
    slots = stage.shape[0]
    devices = wide_count * narrow_count
    face = dofs // 4
    packed = subs * coarse_dofs
    row_pad = wide_rows.shape[3]
    column_pad = coarse_parts.shape[0]
    wide = lax.axis_index("wide")
    narrow = lax.axis_index("narrow")

    def wrapped(position, step, count):
        moved = position + step
        return jnp.where(moved >= count, moved - count, moved)

    west = wrapped(wide, wide_count - 1, wide_count)
    east = wrapped(wide, 1, wide_count)
    south = jnp.maximum(narrow - 1, 0)
    north = jnp.minimum(narrow + 1, narrow_count - 1)
    has_south = narrow > 0
    has_north = narrow < narrow_count - 1
    wide_peers = [(wrapped(wide, step, wide_count), narrow) for step in range(1, wide_count)]
    narrow_peers = [(wide, wrapped(narrow, step, narrow_count)) for step in range(1, narrow_count)]

    def stage_copy(source, s):
        q = s if source is local_ref else s + subs
        slot = lax.rem(q, slots)
        return pltpu.make_async_copy(source.at[s], stage.at[slot], stage_sems.at[slot])

    south_faces[...] = jnp.zeros_like(south_faces)
    north_faces[...] = jnp.zeros_like(north_faces)
    halo_hoop[...] = jnp.zeros_like(halo_hoop)
    halo_across[...] = jnp.zeros_like(halo_across)
    barrier = pltpu.get_barrier_semaphore()
    for peer in wide_peers + narrow_peers:
        pl.semaphore_signal(barrier, inc=1, device_id=peer, device_id_type=MESH)
    fetches = (
        pltpu.make_async_copy(loads_hbm, loads_ref, input_sems.at[0]),
        pltpu.make_async_copy(basis_hbm, basis_ref, input_sems.at[1]),
        pltpu.make_async_copy(coarse_hbm, coarse_ref, input_sems.at[2]),
    )
    for fetch in fetches:
        fetch.start()
    for s in range(slots):
        stage_copy(local_ref, s).start()

    index_row = jnp.concatenate(
        [index_ref[a, b : b + 1] for a in range(sub_circ) for b in range(sub_across)], axis=1
    )
    numbers[pl.ds(wide, 1)] = jnp.broadcast_to(index_row, (1, 8, packed))
    numbers_across[pl.ds(narrow, 1)] = jnp.broadcast_to(index_row, (1, 8, packed))
    pieces_out[...] = jnp.zeros_like(pieces_out)

    pl.semaphore_wait(barrier, len(wide_peers) + len(narrow_peers))

    def remote(src, dst, phase, peer):
        return pltpu.make_async_remote_copy(
            src_ref=src,
            dst_ref=dst,
            send_sem=all_send.at[phase],
            recv_sem=all_recv.at[phase],
            device_id=peer,
            device_id_type=MESH,
        )

    def send(block, phase, peers):
        for peer in peers:
            remote(block, block, phase, peer).start()

    def arrivals(slots, phase, peers):
        part = slots.at[pl.ds(0, len(peers))]
        return remote(part, part, phase, peers[0])

    def face_copies(source, turn):
        def copy(src, dst, send, recv, target):
            return pltpu.make_async_remote_copy(
                src_ref=src,
                dst_ref=dst.at[turn],
                send_sem=face_send.at[turn, send],
                recv_sem=face_recv.at[turn, recv],
                device_id=target,
                device_id_type=MESH,
            )

        to_west = copy(
            source.at[0, :, :, pl.ds(0, face)], high_faces, 0, 1, (west, narrow)
        )
        to_east = copy(
            source.at[sub_circ - 1, :, :, pl.ds(face, face)], low_faces, 1, 0, (east, narrow)
        )
        to_south = copy(
            source.at[:, 0, :, pl.ds(2 * face, face)],
            north_faces,
            2,
            3,
            (wide, south),
        )
        to_north = copy(
            source.at[:, sub_across - 1, :, pl.ds(3 * face, face)],
            south_faces,
            3,
            2,
            (wide, north),
        )
        return to_west, to_east, to_south, to_north

    def halo_copies():
        turn = 2 * ITERS + 1

        def copy(src, dst, send, recv, target):
            return pltpu.make_async_remote_copy(
                src_ref=src,
                dst_ref=dst,
                send_sem=face_send.at[turn, send],
                recv_sem=face_recv.at[turn, recv],
                device_id=target,
                device_id_type=MESH,
            )

        first, last = 0, sub_across - 1
        return (
            copy(basis_hbm.at[0, :, :, pl.ds(0, face)], halo_hoop.at[0], 0, 1, (west, narrow)),
            copy(
                basis_hbm.at[sub_circ - 1, :, :, pl.ds(face, face)],
                halo_hoop.at[sub_circ - 1],
                1,
                0,
                (east, narrow),
            ),
            copy(
                basis_hbm.at[:, first, :, pl.ds(2 * face, face)],
                halo_across.at[:, first],
                2,
                3,
                (wide, south),
            ),
            copy(
                basis_hbm.at[:, last, :, pl.ds(3 * face, face)],
                halo_across.at[:, last],
                3,
                2,
                (wide, north),
            ),
        )

    def send_four(copies):
        to_west, to_east, to_south, to_north = copies
        to_west.start()
        to_east.start()
        pl.when(has_south)(to_south.start)
        pl.when(has_north)(to_north.start)

    def wait_four(copies):
        to_west, to_east, to_south, to_north = copies
        to_west.wait_recv()
        to_east.wait_recv()
        pl.when(has_north)(to_south.wait_recv)
        pl.when(has_south)(to_north.wait_recv)

    def drain_four(copies):
        to_west, to_east, to_south, to_north = copies
        to_west.wait_send()
        to_east.wait_send()
        pl.when(has_south)(to_south.wait_send)
        pl.when(has_north)(to_north.wait_send)

    def summed(source, turn, a, b, extra=None):
        def received(faces, which, i, x, y):
            if extra is None:
                return faces[turn, i]
            start = (x * sub_across + y) * load_count
            return faces[turn, i] + extra[which][start : start + load_count]

        own = source[a, b]
        low = (
            source[a - 1, b, :, face : 2 * face]
            if a > 0
            else received(low_faces, 0, b, sub_circ - 1, b)
        )
        high = (
            source[a + 1, b, :, 0:face]
            if a < sub_circ - 1
            else received(high_faces, 0, b, 0, b)
        )
        below = (
            source[a, b - 1, :, 3 * face :]
            if b > 0
            else received(south_faces, 1, a, a, sub_across - 1)
        )
        above = (
            source[a, b + 1, :, 2 * face : 3 * face]
            if b < sub_across - 1
            else received(north_faces, 1, a, a, 0)
        )
        return own + jnp.concatenate([low, high, below, above], axis=1)

    def inv_mult(b):
        below = jnp.where(has_south, 0.5, 1.0) if b == 0 else 0.5
        above = jnp.where(has_north, 0.5, 1.0) if b == sub_across - 1 else 0.5
        lane = lax.broadcasted_iota(jnp.int32, (1, dofs), 1)
        return jnp.where(lane >= 3 * face, above, jnp.where(lane >= 2 * face, below, 0.5))

    def split_stage(target):
        source = local_ref if target is local_parts else schur_ref

        def body(s, carry):
            stage_copy(source, s).wait()
            high, low = halves(stage[lax.rem(s if source is local_ref else s + subs, slots)])
            target[0, s] = high.astype(BF16)
            target[1, s] = low.astype(BF16)
            later = s + slots
            pl.when(later < subs)(lambda: stage_copy(source, later).start())
            if source is local_ref:
                pl.when(later >= subs)(lambda: stage_copy(schur_ref, later - subs).start())
            return carry

        lax.fori_loop(0, subs, body, 0)

    def apply_block(parts, s, vector):
        out = dot(vector, parts[0, s]) + dot(vector, parts[1, s])
        return out[0:load_count] + out[load_count:]

    send_four(face_copies(loads_hbm, 0))
    send(numbers.at[wide], 0, wide_peers)
    send(numbers_across.at[narrow], 1, narrow_peers)
    send_four(halo_copies())
    fetches[1].wait()
    basis = basis_ref[...].reshape(packed, dofs)
    for target, value in ((basis_parts, basis), (basis_turned, basis.T)):
        high, low = halves(value)
        target[0] = high.astype(BF16)
        target[1] = low.astype(BF16)
    fetches[2].wait()
    coarse_padded[...] = jnp.zeros_like(coarse_padded)
    coarse_padded[0:rows, 0:columns] = coarse_ref[...]
    high, low = halves(coarse_padded[...].T)
    coarse_parts[:, 0:row_pad] = high.astype(BF16)
    coarse_parts[:, row_pad:] = low.astype(BF16)
    split_stage(local_parts)
    fetches[0].wait()

    lane_sub = lax.broadcasted_iota(jnp.int32, (subs, load_count, packed), 2)
    own_sub = lax.broadcasted_iota(jnp.int32, (subs, load_count, packed), 0)
    mine = (lane_sub >= own_sub * coarse_dofs) & (lane_sub < (own_sub + 1) * coarse_dofs)
    groups = wide_count // GROUP
    stored = hot.shape[0] == groups
    hot_ids = lax.broadcasted_iota(jnp.int32, (packed, LANES), 1)

    def fill(group, slot):
        for p in range(GROUP):
            row = numbers[group * GROUP + p, 0:1]
            column = jnp.broadcast_to(row, (LANES, packed)).T
            for tile in range(hot.shape[2] // LANES):
                chosen = (column == hot_ids + tile * LANES).astype(F32).astype(BF16)
                hot[slot, p * packed : (p + 1) * packed, tile * LANES : (tile + 1) * LANES] = chosen

    def make_hot():
        arrivals(numbers, 0, wide_peers).wait_recv()
        if stored:
            for group in range(groups):
                fill(group, group)

    def make_select():
        arrivals(numbers_across, 1, narrow_peers).wait_recv()
        block_ids = lax.broadcasted_iota(jnp.int32, (rows, 3 * packed), 0)
        lane = lax.broadcasted_iota(jnp.int32, (1, packed), 1)
        hoop = jnp.where(
            lane < sub_across * coarse_dofs, numbers[east, 0:1], numbers[west, 0:1]
        )
        lane_across = lax.rem(lane, sub_across * coarse_dofs)
        across = jnp.where(
            lane_across < coarse_dofs, numbers_across[north, 0:1], numbers_across[south, 0:1]
        )
        wanted = jnp.concatenate([numbers[wide, 0:1], hoop, across], axis=1)

        for block in range(wide_count):
            chosen = (block_ids == wanted - block * rows).astype(F32).astype(BF16)
            select[block * rows : (block + 1) * rows] = chosen
        wait_four(halo_copies())
        for source, target in ((halo_hoop, 0), (halo_across, 1)):
            high, low = halves(source[...].reshape(packed, face))
            halo_parts[target, 0] = high.astype(BF16)
            halo_parts[target, 1] = low.astype(BF16)

    def spread(values, parts):
        rows_of = stacked(jnp.where(mine, values[None], 0.0).reshape(subs * load_count, packed))
        out = dot(rows_of, parts[0]) + dot(rows_of, parts[1])
        return out[0 : subs * load_count] + out[subs * load_count :]

    cut = subs // 3

    def smooth(first, last):
        for s in range(first, last):
            smoothed[iteration, s // sub_across, s % sub_across] = apply_block(
                local_parts, s, weighted_parts[s]
            )

    for iteration in range(ITERS):
        turn = 2 * iteration
        phase = 2 + 4 * iteration
        source = loads_ref if iteration == 0 else field.at[iteration - 1]
        coarse_in = gathered.at[iteration]
        wait_four(face_copies(source, turn))
        for a in range(sub_circ):
            for b in range(sub_across):
                weighted = summed(source, turn, a, b) * inv_mult(b)
                weighted_parts[a * sub_across + b] = stacked(weighted)
        flat = weighted_parts[...].reshape(subs * 2 * load_count, dofs)
        products = dot(flat, basis_turned[0]) + dot(flat, basis_turned[1])
        products = products.reshape(subs, 2, load_count, packed)
        products = products[:, 0] + products[:, 1]
        restricted = jnp.sum(jnp.where(mine, products, 0.0), axis=0)
        coarse_in[pl.ds(wide, 1)] = restricted[None]
        send(coarse_in.at[wide], phase, wide_peers)
        if iteration == 0:
            make_hot()
        smooth(0, cut)
        arrivals(coarse_in, phase, wide_peers).wait_recv()

        def add_group(group, total):
            vector = jnp.concatenate([coarse_in[group * GROUP + p] for p in range(GROUP)], axis=1)
            if not stored:
                fill(group, 0)
            return total + dot(stacked(vector), hot[group if stored else 0])

        total = lax.fori_loop(
            0,
            groups,
            add_group,
            jnp.zeros((2 * load_count, hot.shape[2]), F32),
            unroll=groups if stored else 1,
        )
        total = total[0:load_count] + total[load_count:]
        for n in range(narrow_count):
            pieces_out[iteration, n, :, 0:columns] = total[:, n * columns : (n + 1) * columns]
        for peer in narrow_peers:
            remote(
                pieces_out.at[iteration, peer[1]], pieces_in.at[iteration, narrow], phase + 1, peer
            ).start()
        pieces_in[iteration, pl.ds(narrow, 1)] = pieces_out[iteration, pl.ds(narrow, 1)]
        smooth(cut, 2 * cut)
        if iteration == 0:
            make_select()
        arrivals(pieces_in.at[iteration], phase + 1, narrow_peers).wait_recv()
        total = dot(stacked(jnp.sum(pieces_in[iteration], axis=0)), coarse_parts[...])
        total = total[0:load_count] + total[load_count:]
        total = total[:, 0:row_pad] + total[:, row_pad:]
        narrow_rows[iteration, pl.ds(narrow, 1)] = total[None]
        send(narrow_rows.at[iteration, narrow], phase + 2, narrow_peers)
        smooth(2 * cut, subs)
        send_four(face_copies(smoothed.at[iteration], turn + 1))
        arrivals(narrow_rows.at[iteration], phase + 2, narrow_peers).wait_recv()
        wide_rows[iteration, pl.ds(wide, 1)] = jnp.sum(
            narrow_rows[iteration], axis=0, keepdims=True
        )
        send(wide_rows.at[iteration, wide], phase + 3, wide_peers)
        if iteration == 0:
            split_stage(schur_parts)
        wait_four(face_copies(smoothed.at[iteration], turn + 1))
        arrivals(wide_rows.at[iteration], phase + 3, wide_peers).wait_recv()

        coarse = jnp.concatenate(
            [wide_rows[iteration, block, :, 0:rows] for block in range(wide_count)], axis=1
        )
        picked = dot(stacked(coarse), select[...])
        picked = picked[0:load_count] + picked[load_count:]
        inner = spread(picked[:, 0:packed], basis_parts)
        extra = (
            spread(picked[:, packed : 2 * packed], halo_parts[0]),
            spread(picked[:, 2 * packed :], halo_parts[1]),
        )
        for a in range(sub_circ):
            for b in range(sub_across):
                start = (a * sub_across + b) * load_count
                correction[a, b] = smoothed[iteration, a, b] + inner[start : start + load_count]
        to_west, to_east, to_south, to_north = face_copies(field.at[iteration], turn + 2)
        for a in [0, sub_circ - 1, *range(1, sub_circ - 1)]:
            for b in range(sub_across):
                update = summed(correction, turn + 1, a, b, extra) * inv_mult(b)
                if iteration > 0:
                    update = update + solution_ref[a, b]
                solution_ref[a, b] = update
                field[iteration, a, b] = loads_ref[a, b] - apply_block(
                    schur_parts, a * sub_across + b, stacked(update)
                )
            if a == 0:
                to_west.start()
            if a == sub_circ - 1:
                to_east.start()
        pl.when(has_south)(to_south.start)
        pl.when(has_north)(to_north.start)

    last = field.at[ITERS - 1]
    wait_four(face_copies(last, 2 * ITERS))
    for a in range(sub_circ):
        for b in range(sub_across):
            residual_ref[a, b] = summed(last, 2 * ITERS, a, b)

    arrivals(numbers, 0, wide_peers).wait_send()
    arrivals(numbers_across, 1, narrow_peers).wait_send()
    for iteration in range(ITERS):
        phase = 2 + 4 * iteration
        arrivals(gathered.at[iteration], phase, wide_peers).wait_send()
        arrivals(pieces_in.at[iteration], phase + 1, narrow_peers).wait_send()
        arrivals(narrow_rows.at[iteration], phase + 2, narrow_peers).wait_send()
        arrivals(wide_rows.at[iteration], phase + 3, wide_peers).wait_send()
        drain_four(face_copies(smoothed.at[iteration], 2 * iteration + 1))
        drain_four(face_copies(field.at[iteration], 2 * iteration + 2))
    drain_four(face_copies(loads_hbm, 0))
    drain_four(halo_copies())


def hand_on(solution_in, residual_in, solution_out, residual_out):
    solution_out[...] = solution_in[...]
    residual_out[...] = residual_in[...]


def per_device(wide_count, narrow_count, loads, schur, local_inverse, coarse_basis, coarse_inverse, coarse_index):
    sub_circ, sub_across, load_count, dofs = loads.shape
    coarse_dofs = coarse_basis.shape[2]
    rows, columns = coarse_inverse.shape
    subs = sub_circ * sub_across
    packed = subs * coarse_dofs
    devices = wide_count * narrow_count
    face = dofs // 4
    row_pad = pl.cdiv(rows, LANES) * LANES
    column_pad = pl.cdiv(columns, LANES) * LANES
    turns = 2 * ITERS + 1
    slots = subs
    hot_bytes = wide_count * packed * narrow_count * columns * 2
    hot_slots = wide_count // GROUP if hot_bytes <= HOT_BYTES else 1
    dims = (wide_count, narrow_count, sub_circ, sub_across, load_count, dofs, coarse_dofs, rows, columns)
    vmem = pl.BlockSpec(memory_space=pltpu.VMEM)
    anywhere = pl.BlockSpec(memory_space=pl.ANY)
    shape = jax.ShapeDtypeStruct(loads.shape, F32)
    results = (
        pl.pallas_call(
            functools.partial(kernel, dims),
            out_shape=(shape, shape),
            in_specs=[anywhere, anywhere, anywhere, anywhere, anywhere, vmem],
            out_specs=(vmem, vmem),
            scratch_shapes=[
                pltpu.VMEM(loads.shape, F32),
                pltpu.VMEM(coarse_basis.shape, F32),
                pltpu.VMEM(coarse_inverse.shape, F32),
                pltpu.VMEM((row_pad, column_pad), F32),
                pltpu.VMEM((slots, dofs, dofs), F32),
                pltpu.VMEM((2, subs, dofs, dofs), BF16),
                pltpu.VMEM((2, subs, dofs, dofs), BF16),
                pltpu.VMEM((column_pad, 2 * row_pad), BF16),
                pltpu.VMEM((hot_slots, GROUP * packed, pl.cdiv(narrow_count * columns, LANES) * LANES), BF16),
                pltpu.VMEM((wide_count * rows, 3 * packed), BF16),
                pltpu.VMEM((2, packed, dofs), BF16),
                pltpu.VMEM((2, dofs, packed), BF16),
                pltpu.VMEM((2, 2, packed, face), BF16),
                pltpu.VMEM((sub_circ, sub_across, coarse_dofs, face), F32),
                pltpu.VMEM((sub_circ, sub_across, coarse_dofs, face), F32),
                pltpu.VMEM((ITERS, *loads.shape), F32),
                pltpu.VMEM(loads.shape, F32),
                pltpu.VMEM((subs, 2 * load_count, dofs), BF16),
                pltpu.VMEM((ITERS, *loads.shape), F32),
                pltpu.VMEM((turns, sub_across, load_count, face), F32),
                pltpu.VMEM((turns, sub_across, load_count, face), F32),
                pltpu.VMEM((turns, sub_circ, load_count, face), F32),
                pltpu.VMEM((turns, sub_circ, load_count, face), F32),
                pltpu.VMEM((wide_count, 8, packed), jnp.int32),
                pltpu.VMEM((narrow_count, 8, packed), jnp.int32),
                pltpu.VMEM((ITERS, wide_count, load_count, packed), F32),
                pltpu.VMEM((ITERS, narrow_count, load_count, column_pad), F32),
                pltpu.VMEM((ITERS, narrow_count, load_count, column_pad), F32),
                pltpu.VMEM((ITERS, narrow_count, load_count, row_pad), F32),
                pltpu.VMEM((ITERS, wide_count, load_count, row_pad), F32),
                pltpu.SemaphoreType.DMA((slots,)),
                pltpu.SemaphoreType.DMA((3,)),
                pltpu.SemaphoreType.DMA((turns + 1, 4)),
                pltpu.SemaphoreType.DMA((turns + 1, 4)),
                pltpu.SemaphoreType.DMA((4 * ITERS + 2,)),
                pltpu.SemaphoreType.DMA((4 * ITERS + 2,)),
            ],
            compiler_params=pltpu.CompilerParams(
                collective_id=0, has_side_effects=True, vmem_limit_bytes=60 * 1024 * 1024
            ),
        )(
            loads,
            schur.reshape(subs, dofs, dofs),
            local_inverse.reshape(subs, dofs, dofs),
            coarse_basis,
            coarse_inverse,
            coarse_index,
        )
    )
    return tuple(
        pl.pallas_call(
            hand_on,
            out_shape=(shape, shape),
            in_specs=[vmem, vmem],
            out_specs=(vmem, vmem),
            compiler_params=pltpu.CompilerParams(vmem_limit_bytes=60 * 1024 * 1024),
        )(*results)
    )


def solution(mesh):
    return jax.shard_map(
        functools.partial(per_device, mesh.shape["wide"], mesh.shape["narrow"]),
        mesh=mesh,
        in_specs=(
            P("wide", "narrow", None, None),
            P("wide", "narrow", None, None),
            P("wide", "narrow", None, None),
            P("wide", "narrow", None, None),
            P("wide", "narrow"),
            P("wide", "narrow", None),
        ),
        out_specs=(P("wide", "narrow", None, None), P("wide", "narrow", None, None)),
        check_vma=False,
    )
```

```python
import functools

import jax
import jax.numpy as jnp
from jax import lax
from jax.experimental import pallas as pl
from jax.experimental.pallas import tpu as pltpu
from jax.sharding import PartitionSpec as P

ITERS = 2
MESH = pl.DeviceIdType.MESH
F32 = jnp.float32
BF16 = jnp.bfloat16
GROUP = 4
HOT_BYTES = 8 * 1024 * 1024
LANES = 128


def halves(value):
    high = value.astype(BF16).astype(F32)
    return high, value - high


def stacked(value):
    high, low = halves(value)
    return jnp.concatenate([high, low], axis=0).astype(BF16)


def dot(left, right):
    return jnp.dot(left, right, preferred_element_type=F32)


def kernel(
    dims,
    loads_hbm,
    schur_ref,
    local_ref,
    basis_hbm,
    coarse_hbm,
    index_ref,
    solution_ref,
    residual_ref,
    loads_ref,
    basis_ref,
    coarse_ref,
    coarse_padded,
    stage,
    local_parts,
    schur_parts,
    coarse_parts,
    hot,
    select,
    basis_parts,
    basis_turned,
    halo_parts,
    halo_hoop,
    halo_across,
    field,
    correction,
    weighted_parts,
    smoothed,
    low_faces,
    high_faces,
    south_faces,
    north_faces,
    numbers,
    numbers_across,
    gathered,
    pieces_out,
    pieces_in,
    narrow_rows,
    wide_rows,
    stage_sems,
    input_sems,
    face_send,
    face_recv,
    all_send,
    all_recv,
):
    wide_count, narrow_count, sub_circ, sub_across, load_count, dofs, coarse_dofs, rows, columns = dims
    subs = sub_circ * sub_across
    slots = stage.shape[0]
    devices = wide_count * narrow_count
    face = dofs // 4
    packed = subs * coarse_dofs
    row_pad = wide_rows.shape[3]
    column_pad = coarse_parts.shape[0]
    wide = lax.axis_index("wide")
    narrow = lax.axis_index("narrow")

    def wrapped(position, step, count):
        moved = position + step
        return jnp.where(moved >= count, moved - count, moved)

    west = wrapped(wide, wide_count - 1, wide_count)
    east = wrapped(wide, 1, wide_count)
    south = jnp.maximum(narrow - 1, 0)
    north = jnp.minimum(narrow + 1, narrow_count - 1)
    has_south = narrow > 0
    has_north = narrow < narrow_count - 1
    wide_peers = [(wrapped(wide, step, wide_count), narrow) for step in range(1, wide_count)]
    narrow_peers = [(wide, wrapped(narrow, step, narrow_count)) for step in range(1, narrow_count)]

    def stage_copy(source, s):
        q = s if source is local_ref else s + subs
        slot = lax.rem(q, slots)
        return pltpu.make_async_copy(source.at[s], stage.at[slot], stage_sems.at[slot])

    south_faces[...] = jnp.zeros_like(south_faces)
    north_faces[...] = jnp.zeros_like(north_faces)
    halo_hoop[...] = jnp.zeros_like(halo_hoop)
    halo_across[...] = jnp.zeros_like(halo_across)
    barrier = pltpu.get_barrier_semaphore()
    for peer in wide_peers + narrow_peers:
        pl.semaphore_signal(barrier, inc=1, device_id=peer, device_id_type=MESH)
    fetches = (
        pltpu.make_async_copy(loads_hbm, loads_ref, input_sems.at[0]),
        pltpu.make_async_copy(basis_hbm, basis_ref, input_sems.at[1]),
        pltpu.make_async_copy(coarse_hbm, coarse_ref, input_sems.at[2]),
    )
    for fetch in fetches:
        fetch.start()
    for s in range(slots):
        stage_copy(local_ref, s).start()

    index_row = jnp.concatenate(
        [index_ref[a, b : b + 1] for a in range(sub_circ) for b in range(sub_across)], axis=1
    )
    numbers[pl.ds(wide, 1)] = jnp.broadcast_to(index_row, (1, 8, packed))
    numbers_across[pl.ds(narrow, 1)] = jnp.broadcast_to(index_row, (1, 8, packed))
    pieces_out[...] = jnp.zeros_like(pieces_out)

    pl.semaphore_wait(barrier, len(wide_peers) + len(narrow_peers))

    def remote(src, dst, phase, peer):
        return pltpu.make_async_remote_copy(
            src_ref=src,
            dst_ref=dst,
            send_sem=all_send.at[phase],
            recv_sem=all_recv.at[phase],
            device_id=peer,
            device_id_type=MESH,
        )

    def send(block, phase, peers):
        for peer in peers:
            remote(block, block, phase, peer).start()

    def arrivals(slots, phase, peers):
        part = slots.at[pl.ds(0, len(peers))]
        return remote(part, part, phase, peers[0])

    def face_copies(source, turn):
        def copy(src, dst, send, recv, target):
            return pltpu.make_async_remote_copy(
                src_ref=src,
                dst_ref=dst.at[turn],
                send_sem=face_send.at[turn, send],
                recv_sem=face_recv.at[turn, recv],
                device_id=target,
                device_id_type=MESH,
            )

        to_west = copy(
            source.at[0, :, :, pl.ds(0, face)], high_faces, 0, 1, (west, narrow)
        )
        to_east = copy(
            source.at[sub_circ - 1, :, :, pl.ds(face, face)], low_faces, 1, 0, (east, narrow)
        )
        to_south = copy(
            source.at[:, 0, :, pl.ds(2 * face, face)],
            north_faces,
            2,
            3,
            (wide, south),
        )
        to_north = copy(
            source.at[:, sub_across - 1, :, pl.ds(3 * face, face)],
            south_faces,
            3,
            2,
            (wide, north),
        )
        return to_west, to_east, to_south, to_north

    def halo_copies():
        turn = 2 * ITERS + 1

        def copy(src, dst, send, recv, target):
            return pltpu.make_async_remote_copy(
                src_ref=src,
                dst_ref=dst,
                send_sem=face_send.at[turn, send],
                recv_sem=face_recv.at[turn, recv],
                device_id=target,
                device_id_type=MESH,
            )

        first, last = 0, sub_across - 1
        return (
            copy(basis_hbm.at[0, :, :, pl.ds(0, face)], halo_hoop.at[0], 0, 1, (west, narrow)),
            copy(
                basis_hbm.at[sub_circ - 1, :, :, pl.ds(face, face)],
                halo_hoop.at[sub_circ - 1],
                1,
                0,
                (east, narrow),
            ),
            copy(
                basis_hbm.at[:, first, :, pl.ds(2 * face, face)],
                halo_across.at[:, first],
                2,
                3,
                (wide, south),
            ),
            copy(
                basis_hbm.at[:, last, :, pl.ds(3 * face, face)],
                halo_across.at[:, last],
                3,
                2,
                (wide, north),
            ),
        )

    def send_four(copies):
        to_west, to_east, to_south, to_north = copies
        to_west.start()
        to_east.start()
        pl.when(has_south)(to_south.start)
        pl.when(has_north)(to_north.start)

    def wait_four(copies):
        to_west, to_east, to_south, to_north = copies
        to_west.wait_recv()
        to_east.wait_recv()
        pl.when(has_north)(to_south.wait_recv)
        pl.when(has_south)(to_north.wait_recv)

    def drain_four(copies):
        to_west, to_east, to_south, to_north = copies
        to_west.wait_send()
        to_east.wait_send()
        pl.when(has_south)(to_south.wait_send)
        pl.when(has_north)(to_north.wait_send)

    def summed(source, turn, a, b, extra=None):
        def received(faces, which, i, x, y):
            if extra is None:
                return faces[turn, i]
            start = (x * sub_across + y) * load_count
            return faces[turn, i] + extra[which][start : start + load_count]

        own = source[a, b]
        low = (
            source[a - 1, b, :, face : 2 * face]
            if a > 0
            else received(low_faces, 0, b, sub_circ - 1, b)
        )
        high = (
            source[a + 1, b, :, 0:face]
            if a < sub_circ - 1
            else received(high_faces, 0, b, 0, b)
        )
        below = (
            source[a, b - 1, :, 3 * face :]
            if b > 0
            else received(south_faces, 1, a, a, sub_across - 1)
        )
        above = (
            source[a, b + 1, :, 2 * face : 3 * face]
            if b < sub_across - 1
            else received(north_faces, 1, a, a, 0)
        )
        return own + jnp.concatenate([low, high, below, above], axis=1)

    def inv_mult(b):
        below = jnp.where(has_south, 0.5, 1.0) if b == 0 else 0.5
        above = jnp.where(has_north, 0.5, 1.0) if b == sub_across - 1 else 0.5
        lane = lax.broadcasted_iota(jnp.int32, (1, dofs), 1)
        return jnp.where(lane >= 3 * face, above, jnp.where(lane >= 2 * face, below, 0.5))

    def split_stage(target):
        source = local_ref if target is local_parts else schur_ref

        def body(s, carry):
            stage_copy(source, s).wait()
            high, low = halves(stage[lax.rem(s if source is local_ref else s + subs, slots)])
            target[0, s] = high.astype(BF16)
            target[1, s] = low.astype(BF16)
            later = s + slots
            pl.when(later < subs)(lambda: stage_copy(source, later).start())
            if source is local_ref:
                pl.when(later >= subs)(lambda: stage_copy(schur_ref, later - subs).start())
            return carry

        lax.fori_loop(0, subs, body, 0)

    def apply_block(parts, s, vector):
        out = dot(vector, parts[0, s]) + dot(vector, parts[1, s])
        return out[0:load_count] + out[load_count:]

    send_four(face_copies(loads_hbm, 0))
    send(numbers.at[wide], 0, wide_peers)
    send(numbers_across.at[narrow], 1, narrow_peers)
    send_four(halo_copies())
    fetches[1].wait()
    basis = basis_ref[...].reshape(packed, dofs)
    for target, value in ((basis_parts, basis), (basis_turned, basis.T)):
        high, low = halves(value)
        target[0] = high.astype(BF16)
        target[1] = low.astype(BF16)
    fetches[2].wait()
    coarse_padded[...] = jnp.zeros_like(coarse_padded)
    coarse_padded[0:rows, 0:columns] = coarse_ref[...]
    high, low = halves(coarse_padded[...].T)
    coarse_parts[:, 0:row_pad] = high.astype(BF16)
    coarse_parts[:, row_pad:] = low.astype(BF16)
    fetches[0].wait()

    lane_sub = lax.broadcasted_iota(jnp.int32, (subs, load_count, packed), 2)
    own_sub = lax.broadcasted_iota(jnp.int32, (subs, load_count, packed), 0)
    mine = (lane_sub >= own_sub * coarse_dofs) & (lane_sub < (own_sub + 1) * coarse_dofs)
    groups = wide_count // GROUP
    stored = hot.shape[0] == groups
    hot_ids = lax.broadcasted_iota(jnp.int32, (packed, LANES), 1)

    def fill(group, slot):
        for p in range(GROUP):
            row = numbers[group * GROUP + p, 0:1]
            column = jnp.broadcast_to(row, (LANES, packed)).T
            for tile in range(hot.shape[2] // LANES):
                chosen = (column == hot_ids + tile * LANES).astype(F32).astype(BF16)
                hot[slot, p * packed : (p + 1) * packed, tile * LANES : (tile + 1) * LANES] = chosen

    def make_hot():
        arrivals(numbers, 0, wide_peers).wait_recv()
        if stored:
            for group in range(groups):
                fill(group, group)

    def make_select():
        arrivals(numbers_across, 1, narrow_peers).wait_recv()
        block_ids = lax.broadcasted_iota(jnp.int32, (rows, 3 * packed), 0)
        lane = lax.broadcasted_iota(jnp.int32, (1, packed), 1)
        hoop = jnp.where(
            lane < sub_across * coarse_dofs, numbers[east, 0:1], numbers[west, 0:1]
        )
        lane_across = lax.rem(lane, sub_across * coarse_dofs)
        across = jnp.where(
            lane_across < coarse_dofs, numbers_across[north, 0:1], numbers_across[south, 0:1]
        )
        wanted = jnp.concatenate([numbers[wide, 0:1], hoop, across], axis=1)

        for block in range(wide_count):
            chosen = (block_ids == wanted - block * rows).astype(F32).astype(BF16)
            select[block * rows : (block + 1) * rows] = chosen
        wait_four(halo_copies())
        for source, target in ((halo_hoop, 0), (halo_across, 1)):
            high, low = halves(source[...].reshape(packed, face))
            halo_parts[target, 0] = high.astype(BF16)
            halo_parts[target, 1] = low.astype(BF16)

    def spread(values, parts):
        rows_of = stacked(jnp.where(mine, values[None], 0.0).reshape(subs * load_count, packed))
        out = dot(rows_of, parts[0]) + dot(rows_of, parts[1])
        return out[0 : subs * load_count] + out[subs * load_count :]

    cut = subs // 3

    def smooth(first, last):
        for s in range(first, last):
            smoothed[iteration, s // sub_across, s % sub_across] = apply_block(
                local_parts, s, weighted_parts[s]
            )

    for iteration in range(ITERS):
        turn = 2 * iteration
        phase = 2 + 4 * iteration
        source = loads_ref if iteration == 0 else field.at[iteration - 1]
        coarse_in = gathered.at[iteration]
        wait_four(face_copies(source, turn))
        for a in range(sub_circ):
            for b in range(sub_across):
                weighted = summed(source, turn, a, b) * inv_mult(b)
                weighted_parts[a * sub_across + b] = stacked(weighted)
        flat = weighted_parts[...].reshape(subs * 2 * load_count, dofs)
        products = dot(flat, basis_turned[0]) + dot(flat, basis_turned[1])
        products = products.reshape(subs, 2, load_count, packed)
        products = products[:, 0] + products[:, 1]
        restricted = jnp.sum(jnp.where(mine, products, 0.0), axis=0)
        coarse_in[pl.ds(wide, 1)] = restricted[None]
        send(coarse_in.at[wide], phase, wide_peers)
        if iteration == 0:
            split_stage(local_parts)
            make_hot()
        smooth(0, cut)
        arrivals(coarse_in, phase, wide_peers).wait_recv()

        def add_group(group, total):
            vector = jnp.concatenate([coarse_in[group * GROUP + p] for p in range(GROUP)], axis=1)
            if not stored:
                fill(group, 0)
            return total + dot(stacked(vector), hot[group if stored else 0])

        total = lax.fori_loop(
            0,
            groups,
            add_group,
            jnp.zeros((2 * load_count, hot.shape[2]), F32),
            unroll=groups if stored else 1,
        )
        total = total[0:load_count] + total[load_count:]
        for n in range(narrow_count):
            pieces_out[iteration, n, :, 0:columns] = total[:, n * columns : (n + 1) * columns]
        for peer in narrow_peers:
            remote(
                pieces_out.at[iteration, peer[1]], pieces_in.at[iteration, narrow], phase + 1, peer
            ).start()
        pieces_in[iteration, pl.ds(narrow, 1)] = pieces_out[iteration, pl.ds(narrow, 1)]
        smooth(cut, 2 * cut)
        if iteration == 0:
            make_select()
        arrivals(pieces_in.at[iteration], phase + 1, narrow_peers).wait_recv()
        total = dot(stacked(jnp.sum(pieces_in[iteration], axis=0)), coarse_parts[...])
        total = total[0:load_count] + total[load_count:]
        total = total[:, 0:row_pad] + total[:, row_pad:]
        narrow_rows[iteration, pl.ds(narrow, 1)] = total[None]
        send(narrow_rows.at[iteration, narrow], phase + 2, narrow_peers)
        smooth(2 * cut, subs)
        send_four(face_copies(smoothed.at[iteration], turn + 1))
        arrivals(narrow_rows.at[iteration], phase + 2, narrow_peers).wait_recv()
        wide_rows[iteration, pl.ds(wide, 1)] = jnp.sum(
            narrow_rows[iteration], axis=0, keepdims=True
        )
        send(wide_rows.at[iteration, wide], phase + 3, wide_peers)
        if iteration == 0:
            split_stage(schur_parts)
        wait_four(face_copies(smoothed.at[iteration], turn + 1))
        arrivals(wide_rows.at[iteration], phase + 3, wide_peers).wait_recv()

        coarse = jnp.concatenate(
            [wide_rows[iteration, block, :, 0:rows] for block in range(wide_count)], axis=1
        )
        picked = dot(stacked(coarse), select[...])
        picked = picked[0:load_count] + picked[load_count:]
        inner = spread(picked[:, 0:packed], basis_parts)
        extra = (
            spread(picked[:, packed : 2 * packed], halo_parts[0]),
            spread(picked[:, 2 * packed :], halo_parts[1]),
        )
        for a in range(sub_circ):
            for b in range(sub_across):
                start = (a * sub_across + b) * load_count
                correction[a, b] = smoothed[iteration, a, b] + inner[start : start + load_count]
        to_west, to_east, to_south, to_north = face_copies(field.at[iteration], turn + 2)
        for a in [0, sub_circ - 1, *range(1, sub_circ - 1)]:
            for b in range(sub_across):
                update = summed(correction, turn + 1, a, b, extra) * inv_mult(b)
                if iteration > 0:
                    update = update + solution_ref[a, b]
                solution_ref[a, b] = update
                field[iteration, a, b] = loads_ref[a, b] - apply_block(
                    schur_parts, a * sub_across + b, stacked(update)
                )
            if a == 0:
                to_west.start()
            if a == sub_circ - 1:
                to_east.start()
        pl.when(has_south)(to_south.start)
        pl.when(has_north)(to_north.start)

    last = field.at[ITERS - 1]
    wait_four(face_copies(last, 2 * ITERS))
    for a in range(sub_circ):
        for b in range(sub_across):
            residual_ref[a, b] = summed(last, 2 * ITERS, a, b)

    arrivals(numbers, 0, wide_peers).wait_send()
    arrivals(numbers_across, 1, narrow_peers).wait_send()
    for iteration in range(ITERS):
        phase = 2 + 4 * iteration
        arrivals(gathered.at[iteration], phase, wide_peers).wait_send()
        arrivals(pieces_in.at[iteration], phase + 1, narrow_peers).wait_send()
        arrivals(narrow_rows.at[iteration], phase + 2, narrow_peers).wait_send()
        arrivals(wide_rows.at[iteration], phase + 3, wide_peers).wait_send()
        drain_four(face_copies(smoothed.at[iteration], 2 * iteration + 1))
        drain_four(face_copies(field.at[iteration], 2 * iteration + 2))
    drain_four(face_copies(loads_hbm, 0))
    drain_four(halo_copies())


def hand_on(solution_in, residual_in, solution_out, residual_out):
    solution_out[...] = solution_in[...]
    residual_out[...] = residual_in[...]


def per_device(wide_count, narrow_count, loads, schur, local_inverse, coarse_basis, coarse_inverse, coarse_index):
    sub_circ, sub_across, load_count, dofs = loads.shape
    coarse_dofs = coarse_basis.shape[2]
    rows, columns = coarse_inverse.shape
    subs = sub_circ * sub_across
    packed = subs * coarse_dofs
    devices = wide_count * narrow_count
    face = dofs // 4
    row_pad = pl.cdiv(rows, LANES) * LANES
    column_pad = pl.cdiv(columns, LANES) * LANES
    turns = 2 * ITERS + 1
    slots = subs
    hot_bytes = wide_count * packed * narrow_count * columns * 2
    hot_slots = wide_count // GROUP if hot_bytes <= HOT_BYTES else 1
    dims = (wide_count, narrow_count, sub_circ, sub_across, load_count, dofs, coarse_dofs, rows, columns)
    vmem = pl.BlockSpec(memory_space=pltpu.VMEM)
    anywhere = pl.BlockSpec(memory_space=pl.ANY)
    shape = jax.ShapeDtypeStruct(loads.shape, F32)
    results = (
        pl.pallas_call(
            functools.partial(kernel, dims),
            out_shape=(shape, shape),
            in_specs=[anywhere, anywhere, anywhere, anywhere, anywhere, vmem],
            out_specs=(vmem, vmem),
            scratch_shapes=[
                pltpu.VMEM(loads.shape, F32),
                pltpu.VMEM(coarse_basis.shape, F32),
                pltpu.VMEM(coarse_inverse.shape, F32),
                pltpu.VMEM((row_pad, column_pad), F32),
                pltpu.VMEM((slots, dofs, dofs), F32),
                pltpu.VMEM((2, subs, dofs, dofs), BF16),
                pltpu.VMEM((2, subs, dofs, dofs), BF16),
                pltpu.VMEM((column_pad, 2 * row_pad), BF16),
                pltpu.VMEM((hot_slots, GROUP * packed, pl.cdiv(narrow_count * columns, LANES) * LANES), BF16),
                pltpu.VMEM((wide_count * rows, 3 * packed), BF16),
                pltpu.VMEM((2, packed, dofs), BF16),
                pltpu.VMEM((2, dofs, packed), BF16),
                pltpu.VMEM((2, 2, packed, face), BF16),
                pltpu.VMEM((sub_circ, sub_across, coarse_dofs, face), F32),
                pltpu.VMEM((sub_circ, sub_across, coarse_dofs, face), F32),
                pltpu.VMEM((ITERS, *loads.shape), F32),
                pltpu.VMEM(loads.shape, F32),
                pltpu.VMEM((subs, 2 * load_count, dofs), BF16),
                pltpu.VMEM((ITERS, *loads.shape), F32),
                pltpu.VMEM((turns, sub_across, load_count, face), F32),
                pltpu.VMEM((turns, sub_across, load_count, face), F32),
                pltpu.VMEM((turns, sub_circ, load_count, face), F32),
                pltpu.VMEM((turns, sub_circ, load_count, face), F32),
                pltpu.VMEM((wide_count, 8, packed), jnp.int32),
                pltpu.VMEM((narrow_count, 8, packed), jnp.int32),
                pltpu.VMEM((ITERS, wide_count, load_count, packed), F32),
                pltpu.VMEM((ITERS, narrow_count, load_count, column_pad), F32),
                pltpu.VMEM((ITERS, narrow_count, load_count, column_pad), F32),
                pltpu.VMEM((ITERS, narrow_count, load_count, row_pad), F32),
                pltpu.VMEM((ITERS, wide_count, load_count, row_pad), F32),
                pltpu.SemaphoreType.DMA((slots,)),
                pltpu.SemaphoreType.DMA((3,)),
                pltpu.SemaphoreType.DMA((turns + 1, 4)),
                pltpu.SemaphoreType.DMA((turns + 1, 4)),
                pltpu.SemaphoreType.DMA((4 * ITERS + 2,)),
                pltpu.SemaphoreType.DMA((4 * ITERS + 2,)),
            ],
            compiler_params=pltpu.CompilerParams(
                collective_id=0, has_side_effects=True, vmem_limit_bytes=60 * 1024 * 1024
            ),
        )(
            loads,
            schur.reshape(subs, dofs, dofs),
            local_inverse.reshape(subs, dofs, dofs),
            coarse_basis,
            coarse_inverse,
            coarse_index,
        )
    )
    return tuple(
        pl.pallas_call(
            hand_on,
            out_shape=(shape, shape),
            in_specs=[vmem, vmem],
            out_specs=(vmem, vmem),
            compiler_params=pltpu.CompilerParams(vmem_limit_bytes=60 * 1024 * 1024),
        )(*results)
    )


def solution(mesh):
    return jax.shard_map(
        functools.partial(per_device, mesh.shape["wide"], mesh.shape["narrow"]),
        mesh=mesh,
        in_specs=(
            P("wide", "narrow", None, None),
            P("wide", "narrow", None, None),
            P("wide", "narrow", None, None),
            P("wide", "narrow", None, None),
            P("wide", "narrow"),
            P("wide", "narrow", None),
        ),
        out_specs=(P("wide", "narrow", None, None), P("wide", "narrow", None, None)),
        check_vma=False,
    )
```
